128 devices in a mesh: ctx: 16 (over z, x), head: 8 (over y, core).
Axes of the slice: x: 4, y: 4, z: 4, core: 2. Of those that a mesh axis runs over, the one named last changes fastest.
Arguments:
- q_in: bfloat16 [32768, 4096], P(('ctx', 'head')), may hold values from -20 to 20
- kv_in: bfloat16 [32768, 2048], P(('ctx', 'head')), may hold values from -6 to 6
- x_in: bfloat16 [32768, 8192], P(('ctx', 'head')), may hold values from -6 to 6
- z_in: bfloat16 [32768, 8192], P(('ctx', 'head')), may hold values from -6 to 6
- bc_in: bfloat16 [32768, 2048], P(('ctx', 'head')), may hold values from -6 to 6
- dt_in: bfloat16 [32768, 128], P(('ctx', 'head')), may hold values from 0.25 to 2
- conv_x: float32 [4, 8192], P(None, 'head'), may hold values from -3 to 3
- conv_bc: float32 [4, 2048], P(None, 'head'), may hold values from -3 to 3
- a_log: float32 [128], P('head'), as said below
- d_skip: float32 [128], P('head'), may hold values from 0.5 to 2
- norm_gain: float32 [8192], P('head'), may hold values from 0.5 to 1.5
- doc_lengths: int32 [64], replicated, may hold values from 1 to 4096, 32768 in all
- assign: int32 [16, 16], replicated, may hold values from 0 to 15, as said below
Outputs:
- mamba_out: bfloat16 [32768, 8192], P('ctx', 'head')
- attn_out: bfloat16 [32768, 4096], P('ctx', 'head')
The draws below stay inside these ranges and needn't reach their ends.
Inputs may be any that keep to these rules, and one draw needn't show every extreme that they name: `assign`: each row names every ctx index exactly 1 times. exp(a_log) lies between 1 / 65536 and 1 / 32. `doc_lengths`: one document has exactly 4096 positions.
All inputs are finite; a program needn't handle non-finite values.
Results may differ from the reference program's by a relative error of at most 0.0038.
Values may be sent and summed in bfloat16 or wider, within the bound.
A program may use at most 192 MiB of HBM per device.

```python
import math
import jax
import jax.numpy as jnp
import numpy as np
from jax import lax

QUERY_HEADS = 32
KEY_VALUE_HEADS = 8
HEAD_SIZE = 128
MH = 128
MP = 64
NS = 128
G = 8
KCONV = 4
BLK = 128
R = 1
NBLK = 16
PACKED_TOKENS = 32768
KT = 512
MAXDOC = 4096
NDOC = 64
N_CTX = 16


def attention_base(key):
    key_entries = jnp.clip(jax.random.normal(jax.random.fold_in(key, 1), (PACKED_TOKENS, KEY_VALUE_HEADS, 2, HEAD_SIZE), jnp.float32), -6.0, 6.0)
    query_entries = jnp.clip(jax.random.normal(jax.random.fold_in(key, 2), (PACKED_TOKENS, KEY_VALUE_HEADS, QUERY_HEADS // KEY_VALUE_HEADS, HEAD_SIZE), jnp.float32), -6.0, 6.0)
    return (key_entries, query_entries)


def draw_kv_in(key, part):
    key_entries, query_entries = attention_base(key)
    keys_only = key_entries[:, :, 0]
    values_only = key_entries[:, :, 1]
    joined_rows = jnp.stack([keys_only, values_only], axis=2)
    return joined_rows.reshape(PACKED_TOKENS, KEY_VALUE_HEADS * 2 * HEAD_SIZE).astype(jnp.bfloat16)


def draw_q_in(key, part):
    key_entries, query_entries = attention_base(key)
    return query_entries.reshape(PACKED_TOKENS, QUERY_HEADS * HEAD_SIZE).astype(jnp.bfloat16)


def draw_dt_in(key, part):
    key = jax.random.fold_in(key, 29)
    values = jax.random.uniform(key, (PACKED_TOKENS, MH), jnp.float32, 0.5, 1.5)
    return values.astype(jnp.bfloat16)


def draw_a_log(key, part):
    key = jax.random.fold_in(key, 31)
    lowest = math.log(1.0 / (16.0 * MAXDOC))
    highest = math.log(1.0 / 32.0)
    values = jax.random.uniform(key, (MH,), jnp.float32, lowest, highest)
    return values


def draw_assign(key, part):
    key = jax.random.fold_in(key, 37)
    row_keys = jax.random.split(key, N_CTX)
    repeated = jnp.repeat(jnp.arange(N_CTX, dtype=jnp.int32), R)

    def one_row(row_key):
        return jax.random.permutation(row_key, repeated)
    return jax.vmap(one_row)(row_keys).astype(jnp.int32)


def shard_levels(stream_key, dims, shards, least, largest):
    def one(position, shards_of):
        heights = jax.random.uniform(jax.random.fold_in(jax.random.fold_in(stream_key, 6), position), (shards_of,), jnp.float32, least / len(shards), largest / len(shards))
        return jnp.repeat(jnp.exp(heights), dims[position] // shards_of).reshape((-1,) + (1,) * (len(dims) - position - 1))

    gain = one(*shards[0])
    for cut in shards[1:]:
        gain = gain * one(*cut)
    return gain


def split_up(amount, total, most, lean):
    loads = [(1 << 20) // math.isqrt(grade ** lean) + 1 for grade in range(2, amount + 1)]
    spare, holding = total - most - (amount - 1), [1] * (amount - 1)
    while spare > 0:
        movable = [i for i in range(amount - 1) if holding[i] < most]
        pool, remaining = sum([loads[i] for i in movable]), spare
        for i in movable:
            extra = min(most - holding[i], max(1, remaining * loads[i] // pool), spare)
            holding[i] = holding[i] + extra
            spare = spare - extra
    return np.array([most] + holding)


def uneven(key, amount, total, most, slope):
    if amount == 2:
        one = jax.random.randint(key, (), max(1, total - most), min(most, total - 1) + 1)
        return jnp.stack([one, total - one])
    lengths = jnp.asarray(split_up(amount, total, most, slope), jnp.int32)
    pairs = (amount - 1) // 2
    source_of, sink = lengths[1:1 + 2 * pairs:2], lengths[2:2 + 2 * pairs:2]
    margin = jnp.minimum(source_of - 1, most - sink)
    moved = jax.random.randint(jax.random.fold_in(key, 1), (pairs,), 0, 1 << 20) % (margin + 1)
    lengths = lengths.at[1:1 + 2 * pairs:2].set(source_of - moved).at[2:2 + 2 * pairs:2].set(sink + moved)
    return lengths[jax.random.permutation(jax.random.fold_in(key, 2), amount)]


def bell_draw(own_key, dims, spread, reach, cuts=(), kind=jnp.bfloat16):
    values = jax.random.normal(own_key, dims, jnp.float32) * spread
    if len(cuts) > 0:
        values = shard_levels(own_key, dims, cuts, -0.22, 0.18) * values
    return jnp.clip(values, min=-reach, max=reach).astype(kind)


def setup_inputs(seed: int = 0) -> dict:
    seeds = jax.random.split(jax.random.key(seed), 14)
    return {
        "q_in": draw_q_in(jax.random.fold_in(seeds[13], 71), 0),
        "kv_in": draw_kv_in(jax.random.fold_in(seeds[13], 71), 0),
        "x_in": bell_draw(seeds[2], (PACKED_TOKENS, MH * MP), 1.0, 6.0, ((0, 128),)),
        "z_in": bell_draw(seeds[3], (PACKED_TOKENS, MH * MP), 1.0, 6.0, ((0, 128),)),
        "bc_in": bell_draw(seeds[4], (PACKED_TOKENS, G * 2 * NS), 1.0, 6.0, ((0, 128),)),
        "dt_in": draw_dt_in(jax.random.fold_in(seeds[13], 71), 0),
        "conv_x": bell_draw(seeds[6], (KCONV, MH * MP), 0.5, 3.0, ((1, 8),), jnp.float32),
        "conv_bc": bell_draw(seeds[7], (KCONV, G * 2 * NS), 0.5, 3.0, ((1, 8),), jnp.float32),
        "a_log": draw_a_log(jax.random.fold_in(seeds[13], 71), 0),
        "d_skip": jnp.clip(0.5 + 1.5 * jax.random.uniform(seeds[9], (MH,), jnp.float32) ** shard_levels(seeds[9], (MH,), ((0, 8),), -0.2, 0.2), 0.5, 2.0),
        "norm_gain": jnp.clip(1.0 + 0.1 * jax.random.normal(seeds[10], (MH * MP,), jnp.float32), 0.5, 1.5),
        "doc_lengths": uneven(seeds[11], NDOC, PACKED_TOKENS, MAXDOC, 2).astype(jnp.int32),
        "assign": draw_assign(jax.random.fold_in(seeds[13], 71), 0),
    }


EPS = 1e-05
NEG = -1e+30

def doc_index(positions, doc_ends):
    return lax.optimization_barrier(jnp.sum((doc_ends[None, :] <= positions[:, None]).astype(jnp.int32), axis=1))

def masked_conv(raw_rows, taps_weight, positions, start_rows):
    tap_count = taps_weight.shape[0]
    row_count = positions.shape[0]
    running = jnp.zeros((row_count, raw_rows.shape[1]), jnp.float32)
    for tap_index in range(tap_count):
        tap_pos = positions - (tap_count - 1) + tap_index
        inside = tap_pos >= start_rows
        term = raw_rows[tap_index:tap_index + row_count].astype(jnp.float32) * taps_weight[tap_index][None, :]
        running = running + jnp.where(inside[:, None], term, 0.0)
    return jax.nn.silu(running).astype(jnp.bfloat16)

def block_step(carry_state, values_x, values_bc, step_sizes, doc_ids, doc_before, decay_rates, skip_gain):
    half_width = values_bc.shape[-1] // 2
    b_matrix = values_bc[:, :, :half_width].astype(jnp.float32)
    c_matrix = values_bc[:, :, half_width:].astype(jnp.float32)
    cum_log = jnp.cumsum(step_sizes * decay_rates[None], axis=0)
    row_count = doc_ids.shape[0]
    offsets_in = jnp.arange(row_count)
    inside = (doc_ids[:, None] == doc_ids[None, :]) & (offsets_in[:, None] >= offsets_in[None, :])
    intersection = jnp.einsum('tgn,sgn->gts', c_matrix, b_matrix)
    cum_heads = jnp.transpose(cum_log, (1, 2, 0))
    gap_log = cum_heads[:, :, :, None] - cum_heads[:, :, None, :]
    decay_mat = jnp.where(inside, jnp.exp(jnp.where(inside, gap_log, 0.0)), 0.0)
    weights = (intersection[:, None] * decay_mat * jnp.transpose(step_sizes, (1, 2, 0))[:, :, None, :]).astype(jnp.bfloat16)
    within = jnp.einsum('ghts,sghp->tghp', weights.astype(jnp.float32), values_x.astype(jnp.float32))
    joined_rows = doc_ids == doc_before
    lead_in = jnp.where(joined_rows[:, None, None], jnp.exp(cum_log), 0.0)
    carried = jnp.einsum('tgn,ghpn->tghp', c_matrix, carry_state, precision=lax.Precision.HIGHEST)
    output = within + lead_in[..., None] * carried + skip_gain[None, :, :, None] * values_x.astype(jnp.float32)
    same_last = (doc_ids == doc_ids[-1]).astype(jnp.float32)
    tail_w = jnp.exp(cum_log[-1][None] - cum_log) * step_sizes * same_last[:, None, None]
    scaled = (values_x.astype(jnp.float32) * tail_w[..., None]).astype(jnp.bfloat16)
    fresh = jnp.einsum('sghp,sgn->ghpn', scaled.astype(jnp.float32), b_matrix)
    factor = jnp.where(joined_rows[-1], jnp.exp(cum_log[-1]), 0.0)
    return (factor[..., None, None] * carry_state + fresh, output)

def attend_block(query_block, window, window_base, first_row, doc_ends, doc_starts):
    block_rows = query_block.shape[0]
    kv_heads = window.shape[1] // (2 * HEAD_SIZE)
    grouped = query_block.shape[1] // (kv_heads * HEAD_SIZE)
    queries = query_block.reshape(block_rows, kv_heads, grouped, HEAD_SIZE).transpose(1, 2, 0, 3)
    queries = queries.reshape(kv_heads, grouped * block_rows, HEAD_SIZE).astype(jnp.float32)
    q_pos = first_row + jnp.arange(block_rows, dtype=jnp.int32)
    q_doc = doc_index(q_pos, doc_ends)
    flat_pos = jnp.tile(q_pos, grouped)
    flat_doc = jnp.tile(q_doc, grouped)
    doc_first = jnp.max(jnp.where(doc_starts <= first_row, doc_starts, 0))
    tile_first = doc_first // KT
    tile_last = (first_row + block_rows - 1) // KT
    score_scale = 1.0 / math.sqrt(HEAD_SIZE)

    def visit(tile_index, state_tuple):
        run_max, run_sum, run_acc = state_tuple
        offset = tile_index * KT
        key_piece = lax.dynamic_slice_in_dim(window, (offset - window_base).astype(jnp.int32), KT, 0)
        key_piece = key_piece.reshape(KT, kv_heads, 2, HEAD_SIZE).astype(jnp.float32)
        scores = jnp.einsum('gqd,kgd->gqk', queries, key_piece[:, :, 0]) * score_scale
        k_pos = offset + jnp.arange(KT, dtype=jnp.int32)
        k_doc = doc_index(k_pos, doc_ends)
        visible = (k_pos[None, :] <= flat_pos[:, None]) & (k_doc[None, :] == flat_doc[:, None])
        scores = jnp.where(visible[None], scores, NEG)
        new_max = jnp.maximum(run_max, lax.optimization_barrier(jnp.max(scores, axis=-1)))
        probs_tile = jnp.where(visible[None], jnp.exp(scores - new_max[..., None]), 0.0)
        rescale = jnp.exp(run_max - new_max)
        run_sum = run_sum * rescale + lax.optimization_barrier(jnp.sum(probs_tile, axis=-1))
        rounded = probs_tile.astype(jnp.bfloat16).astype(jnp.float32)
        run_acc = run_acc * rescale[..., None] + jnp.einsum('gqk,kgd->gqd', rounded, key_piece[:, :, 1])
        return (new_max, run_sum, run_acc)
    start_tuple = (jnp.full((kv_heads, grouped * block_rows), NEG, jnp.float32), jnp.zeros((kv_heads, grouped * block_rows), jnp.float32), jnp.zeros((kv_heads, grouped * block_rows, HEAD_SIZE), jnp.float32))
    finished = lax.fori_loop(tile_first, tile_last + 1, visit, start_tuple)
    result = finished[2] / finished[1][..., None]
    result = result.reshape(kv_heads, grouped, block_rows, HEAD_SIZE).transpose(2, 0, 1, 3)
    return result.reshape(block_rows, kv_heads * grouped * HEAD_SIZE).astype(jnp.bfloat16)

def reference(q_in, kv_in, x_in, z_in, bc_in, dt_in, conv_x, conv_bc, a_log, d_skip, norm_gain, doc_lengths, assign):
    doc_ends = jnp.cumsum(doc_lengths).astype(jnp.int32)
    doc_starts = (doc_ends - doc_lengths).astype(jnp.int32)
    per_group = MH // G
    block_count = PACKED_TOKENS // BLK
    padded_x = jnp.concatenate([jnp.zeros((KCONV - 1, MH * MP), jnp.bfloat16), x_in], 0)
    padded_bc = jnp.concatenate([jnp.zeros((KCONV - 1, G * 2 * NS), jnp.bfloat16), bc_in], 0)
    decay_rates = -jnp.exp(a_log).reshape(G, per_group)
    skip_gain = d_skip.reshape(G, per_group)
    gain_rows = norm_gain.reshape(1, G, per_group, MP)

    def mamba_block(carry_state, block_index):
        first_row = (block_index * BLK).astype(jnp.int32)
        positions = first_row + jnp.arange(BLK, dtype=jnp.int32)
        doc_ids = doc_index(positions, doc_ends)
        start_rows = lax.optimization_barrier(jnp.max(jnp.where(doc_starts[None, :] <= positions[:, None], doc_starts[None, :], 0), axis=1))
        raw_x = lax.dynamic_slice_in_dim(padded_x, first_row, BLK + KCONV - 1, 0)
        raw_bc = lax.dynamic_slice_in_dim(padded_bc, first_row, BLK + KCONV - 1, 0)
        values_x = masked_conv(raw_x, conv_x, positions, start_rows).reshape(BLK, G, per_group, MP)
        values_bc = masked_conv(raw_bc, conv_bc, positions, start_rows).reshape(BLK, G, 2 * NS)
        step_rows = lax.dynamic_slice_in_dim(dt_in, first_row, BLK, 0).astype(jnp.float32).reshape(BLK, G, per_group)
        doc_before = jnp.where(block_index > 0, doc_index(positions[:1] - 1, doc_ends)[0], -1)
        new_state, ssm_rows = block_step(carry_state, values_x, values_bc, step_rows, doc_ids, doc_before, decay_rates, skip_gain)
        gate_rows = lax.dynamic_slice_in_dim(z_in, first_row, BLK, 0).astype(jnp.float32).reshape(BLK, G, per_group, MP)
        gated = ssm_rows * jax.nn.silu(gate_rows)
        mean_sq = lax.optimization_barrier(jnp.mean(gated * gated, axis=(2, 3), keepdims=True))
        normed = gated * lax.rsqrt(mean_sq + EPS) * gain_rows
        return (new_state, normed.reshape(BLK, MH * MP).astype(jnp.bfloat16))
    zero_state = jnp.zeros((G, per_group, MP, NS), jnp.float32)
    final_state, mamba_rows = lax.scan(mamba_block, zero_state, jnp.arange(block_count, dtype=jnp.int32))
    mamba_out = mamba_rows.reshape(PACKED_TOKENS, MH * MP)
    q_blocks = q_in.reshape(block_count, BLK, QUERY_HEADS * HEAD_SIZE)
    firsts = jnp.arange(block_count, dtype=jnp.int32) * BLK

    def attend_one(pair_in):
        return attend_block(pair_in[0], kv_in, jnp.int32(0), pair_in[1], doc_ends, doc_starts)
    attn_blocks = lax.map(attend_one, (q_blocks, firsts))
    order_all = jnp.argsort(assign, axis=1, stable=True).astype(jnp.int32)
    picked = jnp.arange(N_CTX, dtype=jnp.int32)[:, None, None] * NBLK + order_all.reshape(N_CTX, N_CTX, R)
    picked = jnp.transpose(picked, (1, 0, 2)).reshape(-1)
    attn_out = attn_blocks[picked].reshape(PACKED_TOKENS, QUERY_HEADS * HEAD_SIZE)
    return (mamba_out, attn_out)
```

```python
import functools
import math

import jax
import jax.numpy as jnp
from jax import lax
from jax.experimental import pallas as pl
from jax.experimental.pallas import tpu as pltpu
from jax.sharding import PartitionSpec as P

HEAD_SIZE = 128
MP = 64
NS = 128
BLK = 128
L = 256
EPS = 1e-05
NEG = -1e30
F32 = jnp.float32
BF16 = jnp.bfloat16
VMEM_LIMIT = 56 << 20


def dot(a, b, ca, cb, precision=None):
    return lax.dot_general(
        a, b, (((ca,), (cb,)), ((), ())), preferred_element_type=F32, precision=precision
    )


def silu(v):
    half = 0.5 * v
    return half + half * jnp.tanh(half)


def start_of(pos_col, starts_row):
    return jnp.max(jnp.where(starts_row <= pos_col, starts_row, 0.0), axis=1, keepdims=True)


def column_of_positions(first, count):
    return lax.broadcasted_iota(jnp.int32, (count, 1), 0).astype(F32) + first


def conv(rows, taps, offset):
    count = rows.shape[0] - 16
    total = rows[16:] * taps[3:4]
    for k in range(3):
        term = rows[13 + k : 13 + k + count] * taps[k : k + 1]
        total = total + jnp.where(offset >= float(3 - k), term, 0.0)
    return silu(total)


def head_lanes(heads, width):
    lane = lax.broadcasted_iota(jnp.int32, (heads, width), 1) // MP
    row = lax.broadcasted_iota(jnp.int32, (heads, width), 0)
    return (lane == row).astype(F32).astype(BF16)


def expand(values_t, lanes2):
    hi = values_t.astype(BF16)
    lo = (values_t - hi.astype(F32)).astype(BF16)
    return dot(jnp.concatenate([hi, lo], 0), lanes2, 0, 0)


def decay_sums(dt_t, a_col):
    count = dt_t.shape[1]
    row = lax.broadcasted_iota(jnp.int32, (count, count), 0)
    col = lax.broadcasted_iota(jnp.int32, (count, count), 1)
    upper = (row <= col).astype(F32)
    return dot(-jnp.exp(a_col) * dt_t, upper, 1, 0, lax.Precision.HIGHEST)


def fresh_state(xc, b_rows, dt_t, cum_t, lanes2, pos, start):
    count = xc.shape[0]
    scaled = (xc.astype(F32) * expand(jnp.exp(-cum_t) * dt_t, lanes2)).astype(BF16)
    growth = expand(jnp.exp(cum_t), lanes2)
    b_last = jnp.where(pos >= start[count - 1 :], b_rows.astype(F32), 0.0).astype(BF16)
    return scaled, growth, dot(b_last, scaled, 0, 0)


def chunk_output(xc, b_rows, c_rows, scaled, growth, state, pos, start, first, skip_lanes):
    count = xc.shape[0]
    row = lax.broadcasted_iota(jnp.int32, (count, count), 0)
    col = lax.broadcasted_iota(jnp.int32, (count, count), 1)
    inside = (col <= row) & (col.astype(F32) >= start - first)
    pairs = jnp.where(inside, dot(c_rows, b_rows, 1, 1), 0.0).astype(BF16)
    c_joined = jnp.where(start < first, c_rows.astype(F32), 0.0).astype(BF16)
    hi = state.astype(BF16)
    lo = (state - hi.astype(F32)).astype(BF16)
    mixed = dot(
        jnp.concatenate([pairs, c_joined, c_joined], 1),
        jnp.concatenate([scaled, hi, lo], 0),
        1,
        0,
    )
    return mixed * growth + skip_lanes * xc.astype(F32)


def gate_norm(ssm, z, gain):
    gated = ssm * silu(z.astype(F32))
    mean_sq = jnp.mean(gated * gated, axis=1, keepdims=True)
    return (gated * lax.rsqrt(mean_sq + EPS) * gain).astype(BF16)


def state_kernel(
    starts, x, bc, rim_x, rim_bc, dt_t, a_col, taps_x, taps_bc, xc_out, bcc_out, state_out, thr_out,
    tail_x, tail_bc, state, thr,
):
    j = pl.program_id(0)
    first = ((lax.axis_index("ctx") * 8 + j) * L).astype(F32)
    heads = a_col.shape[0]
    lanes = head_lanes(heads, x.shape[1])
    lanes2 = jnp.concatenate([lanes, lanes], 0)

    @pl.when(j == 0)
    def _():
        tail_x[...] = rim_x[...]
        tail_bc[...] = rim_bc[...]
        state[...] = jnp.zeros_like(state)
        thr[...] = jnp.ones_like(thr)

    pos = column_of_positions(first, L)
    start = start_of(pos, starts[...])
    offset = pos - start
    rows_x = jnp.concatenate([tail_x[...], x[...]], 0).astype(F32)
    rows_bc = jnp.concatenate([tail_bc[...], bc[...]], 0).astype(F32)
    tail_x[...] = x[L - 16 :, :]
    tail_bc[...] = bc[L - 16 :, :]
    xc = conv(rows_x, taps_x[...], offset).astype(BF16)
    bcc = conv(rows_bc, taps_bc[...], offset).astype(BF16)
    xc_out[...] = xc
    bcc_out[...] = bcc
    cum_t = decay_sums(dt_t[...], a_col[...])
    _, growth, fresh = fresh_state(xc, bcc[:, :NS], dt_t[...], cum_t, lanes2, pos, start)
    factor = jnp.where(start[L - 1 :] < first, 1.0, 0.0) * growth[L - 1 :]
    state[...] = factor * state[...] + growth[L - 1 :] * fresh
    thr[...] = factor * thr[...]
    state_out[...] = state[...]
    thr_out[...] = thr[...]


def output_kernel(
    starts, xc, bcc, dt_t, a_col, z, skip, gain, near, far, near_thr, out, state,
):
    j = pl.program_id(0)
    first = ((lax.axis_index("ctx") * 8 + j) * L).astype(F32)
    heads = a_col.shape[0]
    lanes = head_lanes(heads, xc.shape[1])
    lanes2 = jnp.concatenate([lanes, lanes], 0)

    @pl.when(j == 0)
    def _():
        state[...] = near[...] + near_thr[...] * far[...]

    pos = column_of_positions(first, L)
    start = start_of(pos, starts[...])
    cum_t = decay_sums(dt_t[...], a_col[...])
    x = xc[...]
    b_rows, c_rows = bcc[:, :NS], bcc[:, NS:]
    scaled, growth, fresh = fresh_state(x, b_rows, dt_t[...], cum_t, lanes2, pos, start)
    entering = state[...]
    ssm = chunk_output(
        x, b_rows, c_rows, scaled, growth, entering, pos, start, first, skip[...]
    )
    out[...] = gate_norm(ssm, z[...], gain[...])
    joined = jnp.where(start[L - 1 :] < first, 1.0, 0.0)
    state[...] = growth[L - 1 :] * (joined * entering + fresh)


def mamba(starts, x, bc, dt_t, a_col, taps_x, taps_bc, z, skip, gain):
    rows, width = x.shape
    chunks = rows // L
    heads = a_col.shape[0]
    rim_x = ring(x[rows - 16 :], 1)
    rim_bc = ring(bc[rows - 16 :], 1)
    whole = lambda a: pl.BlockSpec(a.shape, lambda j: (0,) * a.ndim)
    by_row = lambda w: pl.BlockSpec((L, w), lambda j: (j, 0))
    by_col = pl.BlockSpec((heads, L), lambda j: (0, j))
    xc, bcc, state, thr = pl.pallas_call(
        state_kernel,
        grid=(chunks,),
        out_shape=(
            jax.ShapeDtypeStruct(x.shape, BF16),
            jax.ShapeDtypeStruct(bc.shape, BF16),
            jax.ShapeDtypeStruct((NS, width), F32),
            jax.ShapeDtypeStruct((1, width), F32),
        ),
        in_specs=[
            whole(starts), by_row(width), by_row(bc.shape[1]), whole(rim_x), whole(rim_bc), by_col,
            whole(a_col), whole(taps_x), whole(taps_bc),
        ],
        out_specs=(
            by_row(width),
            by_row(bc.shape[1]),
            pl.BlockSpec((NS, width), lambda j: (0, 0)),
            pl.BlockSpec((1, width), lambda j: (0, 0)),
        ),
        scratch_shapes=[
            pltpu.VMEM((16, width), BF16),
            pltpu.VMEM((16, bc.shape[1]), BF16),
            pltpu.VMEM((NS, width), F32),
            pltpu.VMEM((1, width), F32),
        ],
        compiler_params=pltpu.CompilerParams(vmem_limit_bytes=VMEM_LIMIT),
        cost_estimate=pl.CostEstimate(flops=2 << 30, bytes_accessed=12 << 20, transcendentals=4 << 20),
        name="mamba_state",
    )(starts, x, bc, rim_x, rim_bc, dt_t, a_col, taps_x, taps_bc)
    near, near_thr = ring(state, 1), ring(thr, 1)
    far = ring(state, 2)
    return pl.pallas_call(
        output_kernel,
        grid=(chunks,),
        out_shape=jax.ShapeDtypeStruct(x.shape, BF16),
        in_specs=[
            whole(starts), by_row(width), by_row(bc.shape[1]), by_col, whole(a_col), by_row(width),
            whole(skip), whole(gain), whole(near), whole(far), whole(near_thr),
        ],
        out_specs=by_row(width),
        scratch_shapes=[pltpu.VMEM((NS, width), F32)],
        compiler_params=pltpu.CompilerParams(vmem_limit_bytes=VMEM_LIMIT),
        cost_estimate=pl.CostEstimate(flops=4 << 30, bytes_accessed=16 << 20, transcendentals=4 << 20),
        name="mamba_output",
    )(starts, xc, bcc, dt_t, a_col, z, skip, gain, near, far, near_thr)


def ring(block, distance):
    count = lax.axis_size("ctx")
    return lax.ppermute(block, "ctx", [(i, (i + distance) % count) for i in range(count)])


TILE = 512
SCALE2 = math.log2(math.e) / math.sqrt(HEAD_SIZE)


def attend(q_rows, b, first, starts, ends, kv, mask, tile_count, acc, top):
    groups = q_rows.shape[1] // HEAD_SIZE
    queries = jnp.concatenate(
        [q_rows[:, i * HEAD_SIZE : (i + 1) * HEAD_SIZE] for i in range(groups)], 0
    )
    pos = column_of_positions(first, BLK)
    own = ((pos >= starts) & (pos < ends)).astype(F32).astype(BF16)
    queries = jnp.concatenate([queries, jnp.concatenate([own] * groups, 0)], 1)
    here = 4096 + b * BLK

    def scores_of(at, count):
        keys = jnp.concatenate([kv[pl.ds(at, count), :HEAD_SIZE], mask[pl.ds(at, count), :]], 1)
        return dot(queries, keys, 1, 1)

    def mixed(probs, at, count):
        values = jnp.concatenate(
            [kv[pl.ds(at, count), HEAD_SIZE:], jnp.ones((count, HEAD_SIZE), BF16)], 1
        )
        return dot(probs.astype(BF16), values, 1, 0)

    at = pl.multiple_of(here, BLK)
    s = scores_of(at, BLK)
    row = lax.broadcasted_iota(jnp.int32, s.shape, 0) % BLK
    col = lax.broadcasted_iota(jnp.int32, s.shape, 1)
    s = jnp.where(col <= row, s, NEG)
    peak = jnp.max(s, axis=1, keepdims=True)
    acc[...] = mixed(jnp.exp2((s - peak) * SCALE2), at, BLK)
    top[...] = peak

    def step(i, _):
        at = pl.multiple_of(here - (i + 1) * TILE, BLK)
        s = scores_of(at, TILE)
        old = top[...]
        new = jnp.maximum(old, jnp.max(s, axis=1, keepdims=True))
        probs = jnp.exp2((s - new) * SCALE2)
        acc[...] = acc[...] * jnp.exp2((old - new) * SCALE2) + mixed(probs, at, TILE)
        top[...] = new
        return 0

    lax.fori_loop(0, tile_count, step, 0)
    total = acc[...]
    out = total[:, :HEAD_SIZE] / total[:, HEAD_SIZE:]
    return jnp.concatenate([out[i * BLK : (i + 1) * BLK] for i in range(groups)], 1).astype(BF16)


def mask_rows(first, count, starts, ends):
    pos = column_of_positions(first, count)
    return jnp.where((pos >= starts) & (pos < ends), 0.0, NEG).astype(BF16)


def attention_kernel(order, tiles, starts, ends, q, far, near, own, out, kv, mask, acc, top):
    j = pl.program_id(0)
    c = lax.axis_index("ctx")
    rows = own.shape[0]

    @pl.when(j == 0)
    def _():
        kv[:rows] = far[...]
        kv[rows : 2 * rows] = near[...]
        kv[2 * rows :] = own[...]

        def fill(i, _):
            at = pl.multiple_of(i * 256, 256)
            first = ((c - 2) * rows + i * 256).astype(F32)
            mask[pl.ds(at, 256), :] = mask_rows(first, 256, starts[...], ends[...])
            return 0

        lax.fori_loop(0, 3 * rows // 256, fill, 0)

    b = order[j]
    first = (c * rows + b * BLK).astype(F32)
    out[...] = attend(q[...], b, first, starts[...], ends[...], kv, mask, tiles[b], acc, top)


def attention(order, tiles, starts, ends, q, far, near, own):
    rows, width = q.shape
    groups = width // HEAD_SIZE
    whole = lambda a: pl.BlockSpec(a.shape, lambda j, o, t: (0,) * a.ndim)
    return pl.pallas_call(
        attention_kernel,
        out_shape=jax.ShapeDtypeStruct(q.shape, BF16),
        grid_spec=pltpu.PrefetchScalarGridSpec(
            num_scalar_prefetch=2,
            grid=(rows // BLK,),
            in_specs=[
                whole(starts), whole(ends),
                pl.BlockSpec((BLK, width), lambda j, o, t: (o[j], 0)),
                whole(far), whole(near), whole(own),
            ],
            out_specs=pl.BlockSpec((BLK, width), lambda j, o, t: (j, 0)),
            scratch_shapes=[
                pltpu.VMEM((3 * rows, own.shape[1]), BF16),
                pltpu.VMEM((3 * rows, 128), BF16),
                pltpu.VMEM((groups * BLK, 2 * HEAD_SIZE), F32),
                pltpu.VMEM((groups * BLK, 1), F32),
            ],
        ),
        compiler_params=pltpu.CompilerParams(vmem_limit_bytes=VMEM_LIMIT),
        cost_estimate=pl.CostEstimate(flops=24 << 30, bytes_accessed=8 << 20, transcendentals=24 << 20),
        name="attention",
    )(order, tiles, starts, ends, q, far, near, own)


def doc_rows(doc_lengths):
    count = doc_lengths.shape[0]
    before = jnp.arange(count)[None, :] < jnp.arange(count)[:, None]
    starts = jnp.sum(jnp.where(before, doc_lengths[None, :], 0), axis=1)
    pad = (0, 128 - count)
    starts_row = jnp.pad(starts.astype(F32), pad, constant_values=1e9)[None]
    ends_row = jnp.pad((starts + doc_lengths).astype(F32), pad, constant_values=1e9)[None]
    return starts, starts_row, ends_row


def shards(
    q_in, kv_in, x_in, z_in, bc_in, dt_in, conv_x, conv_bc, a_log, d_skip, norm_gain, doc_lengths, assign
):
    swap = lambda a: lax.all_to_all(a, "head", split_axis=1, concat_axis=0, tiled=True)
    kv, q = swap(kv_in), swap(q_in)
    bc, dt = swap(bc_in), swap(dt_in)
    x = swap(x_in)
    z = swap(z_in)
    c = lax.axis_index("ctx")
    n_ctx = lax.axis_size("ctx")
    rows = q.shape[0]
    blocks = rows // BLK
    starts, starts_row, ends_row = doc_rows(doc_lengths)
    order = jnp.argsort(lax.dynamic_index_in_dim(assign, c, 0, keepdims=False)).astype(jnp.int32)
    firsts = c * rows + jnp.arange(blocks, dtype=jnp.int32) * BLK
    doc_first = jnp.max(
        jnp.where(starts[None, :] <= firsts[:, None], starts[None, :], 0), axis=1
    )
    tiles = ((firsts - doc_first + TILE - 1) // TILE).astype(jnp.int32)
    mine = attention(order, tiles, starts_row, ends_row, q, ring(kv, 2), ring(kv, 1), kv)
    attn = lax.all_to_all(
        mine.reshape(n_ctx, blocks // n_ctx * BLK, q.shape[1]), "ctx", 0, 0, tiled=True
    ).reshape(rows, q.shape[1])
    skip = jnp.repeat(d_skip, MP)[None]
    mamba_out = mamba(
        starts_row, x, bc, dt.T.astype(F32), a_log[:, None], conv_x, conv_bc, z, skip, norm_gain[None]
    )
    return mamba_out, attn


def solution(mesh):
    rows = P(("ctx", "head"), None)
    return jax.shard_map(
        shards,
        mesh=mesh,
        in_specs=(rows,) * 6 + (P(None, "head"),) * 2 + (P("head"),) * 3 + (P(), P()),
        out_specs=(P("ctx", "head"), P("ctx", "head")),
        check_vma=False,
    )
```

```python
import functools
import math

import jax
import jax.numpy as jnp
from jax import lax
from jax.experimental import pallas as pl
from jax.experimental.pallas import tpu as pltpu
from jax.sharding import PartitionSpec as P

HEAD_SIZE = 128
MP = 64
NS = 128
BLK = 128
L = 256
EPS = 1e-05
NEG = -1e30
F32 = jnp.float32
BF16 = jnp.bfloat16
VMEM_LIMIT = 60 << 20
MESH = pl.DeviceIdType.MESH
TILE = 1024
WINDOW = 4096
SCALE2 = math.log2(math.e) / math.sqrt(HEAD_SIZE)
MSG = NS + 16


def dot(a, b, ca, cb, precision=None):
    return lax.dot_general(
        a, b, (((ca,), (cb,)), ((), ())), preferred_element_type=F32, precision=precision
    )


def silu(v):
    half = 0.5 * v
    return half + half * jnp.tanh(half)


def start_of(pos_col, starts_row):
    return jnp.max(jnp.where(starts_row <= pos_col, starts_row, 0.0), axis=1, keepdims=True)


def column_of_positions(first, count):
    return lax.broadcasted_iota(jnp.int32, (count, 1), 0).astype(F32) + first


def conv(rows, taps, offset):
    count = rows.shape[0] - 16
    total = rows[16:] * taps[3]
    for k in range(3):
        term = rows[13 + k : 13 + k + count] * taps[k]
        total = total + jnp.where(offset >= float(3 - k), term, 0.0)
    return silu(total)


def head_lanes(heads, width):
    lane = lax.broadcasted_iota(jnp.int32, (heads, width), 1) // MP
    row = lax.broadcasted_iota(jnp.int32, (heads, width), 0)
    return (lane == row).astype(F32)


def expand(values_t, lanes2):
    hi = values_t.astype(BF16)
    lo = (values_t - hi.astype(F32)).astype(BF16)
    return dot(jnp.concatenate([hi, lo], 0), lanes2, 0, 0)


def gate_norm(ssm, z, gain):
    gated = ssm * silu(z.astype(F32))
    mean_sq = jnp.mean(gated * gated, axis=1, keepdims=True)
    return (gated * lax.rsqrt(mean_sq + EPS) * gain).astype(BF16)


def put_message(ref, state, factor):
    ref[:NS] = state.astype(BF16)
    hi = factor.astype(BF16).astype(F32)
    row = lax.broadcasted_iota(jnp.int32, (16, state.shape[1]), 0)
    ref[NS:] = jnp.where(row == 0, hi, jnp.where(row == 1, factor - hi, 0.0)).astype(BF16)


def get_message(ref):
    tail = ref[NS:].astype(F32)
    return ref[:NS].astype(F32), tail[0:1] + tail[1:2]


def attend(q_rows, here, first, starts, ends, kv, mask):
    groups = q_rows.shape[1] // HEAD_SIZE
    queries = jnp.concatenate(
        [q_rows[:, i * HEAD_SIZE : (i + 1) * HEAD_SIZE] for i in range(groups)], 0
    )
    pos = column_of_positions(first, BLK)
    own = ((pos >= starts) & (pos < ends)).astype(F32).astype(BF16)
    queries = jnp.concatenate([queries, jnp.concatenate([own] * groups, 0)], 1)

    def scores_of(at, count):
        keys = [jnp.concatenate([kv[at + i][:, :HEAD_SIZE], mask[at + i]], 1) for i in range(count)]
        return dot(queries, jnp.concatenate(keys, 0), 1, 1)

    def mixed(probs, at, count):
        ones = jnp.ones((BLK, HEAD_SIZE), BF16)
        values = [jnp.concatenate([kv[at + i][:, HEAD_SIZE:], ones], 1) for i in range(count)]
        return dot(probs.astype(BF16), jnp.concatenate(values, 0), 1, 0)

    s = scores_of(here, 1)
    row = lax.broadcasted_iota(jnp.int32, s.shape, 0) % BLK
    col = lax.broadcasted_iota(jnp.int32, s.shape, 1)
    s = jnp.where(col <= row, s, NEG)
    peak = jnp.max(s, axis=1, keepdims=True)
    total = mixed(jnp.exp2((s - peak) * SCALE2), here, 1)
    for i in range(WINDOW // TILE):
        at = here - (i + 1) * (TILE // BLK)
        s = scores_of(at, TILE // BLK)
        new = jnp.maximum(peak, jnp.max(s, axis=1, keepdims=True))
        probs = jnp.exp2((s - new) * SCALE2)
        total = total * jnp.exp2((peak - new) * SCALE2) + mixed(probs, at, TILE // BLK)
        peak = new
    out = total[:, :HEAD_SIZE] / total[:, HEAD_SIZE:]
    return jnp.concatenate([out[i * BLK : (i + 1) * BLK] for i in range(groups)], 1).astype(BF16)


def remote(src, dst, sems, slot, device):
    return pltpu.make_async_remote_copy(
        src, dst, sems.at[0, slot], sems.at[1, slot], device_id=device, device_id_type=MESH
    )


def layer_kernel(
    order, q_in, kv_in, x_in, z_in, bc_in, dt_in, conv_x, conv_bc, a_log, d_skip, norm_gain, starts, ends,
    mamba_out, attn_out,
    xbuf, zbuf, bcbuf, xc, scaled, bcc, par, dt_t, cum_t, inside, own_s, own_f, pair_tx, pair_rx, part_tx,
    part_rx, ctx_tx, near, far, ret_tx, ret_rx, back_tx, entering, kv, mask, q, out_tx, attn_tx,
    local, s_kv, s_q, s_par, s_rim, s_halo, s_pair, s_part, s_ctx, s_ret, s_back, s_out, s_attn,
):
    c = lax.axis_index("ctx")
    h = lax.axis_index("head")
    n_ctx, n_head = 16, 8
    y, k = h // 2, h % 2
    rows, width = 256, 1024
    shard = rows * n_head
    nh, nc = lax.rem(h + 1, n_head), lax.rem(c + (h + 1) // n_head, n_ctx)
    ph, pc = lax.rem(h + n_head - 1, n_head), lax.rem(c + n_ctx - (n_head - h) // n_head, n_ctx)
    head_of = lambda o: lax.rem(h + o, n_head)
    ctx_of = lambda o: lax.rem(c + o, n_ctx)

    x_load = pltpu.make_async_copy(x_in, xbuf.at[pl.ds(16, rows)], local.at[0])
    bc_load = pltpu.make_async_copy(bc_in, bcbuf.at[pl.ds(16, rows)], local.at[1])
    z_load = pltpu.make_async_copy(z_in, zbuf, local.at[2])
    mine = pl.ds(pl.multiple_of(h * rows, rows), rows)
    q_mine = pl.ds(2 * h, 2)
    kv_mine = pl.ds(WINDOW // BLK + 2 * h, 2)
    q_load = pltpu.make_async_copy(
        q_in.at[:, :, pl.ds(pl.multiple_of(h * 512, 512), 512)], q.at[q_mine], local.at[3]
    )
    kv_load = pltpu.make_async_copy(
        kv_in.at[:, :, pl.ds(pl.multiple_of(h * 256, 256), 256)], kv.at[kv_mine], local.at[4]
    )
    bc_load.start()
    x_load.start()
    kv_load.start()
    q_load.start()
    z_load.start()

    barrier = pltpu.get_barrier_semaphore()
    for o in range(1, n_head):
        pl.semaphore_signal(barrier, inc=1, device_id=(c, head_of(o)), device_id_type=MESH)
    for o in range(1, n_ctx):
        pl.semaphore_signal(barrier, inc=1, device_id=(ctx_of(o), h), device_id_type=MESH)
    pl.semaphore_signal(barrier, inc=1, device_id=(nc, nh), device_id_type=MESH)
    pl.semaphore_signal(barrier, inc=1, device_id=(pc, ph), device_id_type=MESH)

    lanes = head_lanes(16, width)
    lanes2 = jnp.concatenate([lanes, lanes], 0).astype(BF16)
    par[pl.ds(h, 1)] = jnp.zeros((1, 8, width), F32)
    own_par = par.at[h]
    own_par[0:4] = conv_x[...]
    own_par[4:5] = norm_gain[...]
    for i in range(4):
        own_par[5:6, i * 256 : (i + 1) * 256] = conv_bc[i : i + 1]
    skip8 = jnp.broadcast_to(d_skip[...], (8, 16))
    own_par[6:7] = dot(skip8, lanes, 1, 0, lax.Precision.HIGHEST)[0:1]
    own_par[7:8, 0:16] = a_log[...]
    dt_t[...] = jnp.transpose(dt_in[...].astype(F32))

    first = (c * shard + h * rows).astype(F32)
    pos = column_of_positions(first, rows)
    start = start_of(pos, starts[...])
    offset = pos - start
    row = lax.broadcasted_iota(jnp.int32, (rows, rows), 0)
    col = lax.broadcasted_iota(jnp.int32, (rows, rows), 1)
    inside[...] = ((col <= row) & (col.astype(F32) >= start - first)).astype(F32)
    joined = start < first
    joined_last = jnp.where(start[rows - 1 :] < first, 1.0, 0.0)
    in_last = pos >= start[rows - 1 :]

    pl.semaphore_wait(barrier, n_head - 1 + n_ctx - 1 + 2)

    rims = [
        remote(x_in.at[pl.ds(rows - 16, 16)], xbuf.at[pl.ds(0, 16)], s_rim, 0, (nc, nh)),
        remote(bc_in.at[pl.ds(rows - 16, 16)], bcbuf.at[pl.ds(0, 16)], s_rim, 1, (nc, nh)),
    ]
    pars = [remote(par.at[h], par.at[h], s_par, o, (c, head_of(o))) for o in range(1, n_head)]
    kvs = [
        remote(
            kv_in.at[:, :, pl.ds(pl.multiple_of(head_of(o) * 256, 256), 256)],
            kv.at[kv_mine], s_kv, o, (c, head_of(o)),
        )
        for o in range(1, n_head)
    ]
    qs = [
        remote(
            q_in.at[:, :, pl.ds(pl.multiple_of(head_of(o) * 512, 512), 512)],
            q.at[q_mine], s_q, o, (c, head_of(o)),
        )
        for o in range(1, n_head)
    ]
    for cp in rims + pars + kvs:
        cp.start()
    for cp in pars:
        cp.wait_recv()
    a_col = jnp.concatenate(
        [jnp.transpose(par[g, :, 0:128])[0:16, 7:8] for g in range(n_head)], 0
    )
    upper = (row <= col).astype(F32)
    cum_t[...] = dot(-jnp.exp(a_col) * dt_t[...], upper, 1, 0, lax.Precision.HIGHEST)
    bc_load.wait()
    x_load.wait()
    for cp in rims:
        cp.wait_recv()

    def local_state(g):
        lanes_g = pl.ds(pl.multiple_of(g * width, width), width)
        p = par[g]
        x_rows = conv(
            xbuf[:, lanes_g].astype(F32), [p[i : i + 1] for i in range(4)], offset
        ).astype(BF16)
        bc_rows = conv(
            bcbuf[:, pl.ds(pl.multiple_of(g * 256, 256), 256)].astype(F32),
            [p[5:6, i * 256 : (i + 1) * 256] for i in range(4)],
            offset,
        )
        xc[g] = x_rows
        bcc[g] = bc_rows.astype(BF16)
        heads = pl.ds(pl.multiple_of(g * 16, 16), 16)
        cum = cum_t[heads, :]
        x_scaled = (x_rows.astype(F32) * expand(jnp.exp(-cum) * dt_t[heads, :], lanes2)).astype(BF16)
        scaled[g] = x_scaled
        growth = expand(jnp.exp(cum[:, rows - 128 :]), lanes2)[127:128]
        b_last = jnp.where(in_last, bc_rows[:, :NS], 0.0).astype(BF16)
        return growth * dot(b_last, x_scaled, 0, 0), growth * joined_last

    def other_side(i, _):
        put_message(pair_tx.at[i], *local_state(4 * (1 - k) + i))
        return 0

    def own_side(i, _):
        state, factor = local_state(4 * k + i)
        own_s[i] = state
        own_f[i] = factor
        return 0

    partner = (c, 2 * y + (1 - k))
    lax.fori_loop(0, 4, other_side, 0)
    pair = remote(pair_tx, pair_rx, s_pair, 0, partner)
    pair.start()
    lax.fori_loop(0, 4, own_side, 0)
    pair.wait_recv()

    def join(i, _):
        got_s, got_f = get_message(pair_rx.at[i])
        s1, f1 = jnp.where(k == 0, own_s[i], got_s), jnp.where(k == 0, own_f[i], got_f)
        s2, f2 = jnp.where(k == 0, got_s, own_s[i]), jnp.where(k == 0, got_f, own_f[i])
        put_message(part_tx.at[i], f2 * s1 + s2, f2 * f1)
        own_s[i] = s1
        own_f[i] = f1
        return 0

    lax.fori_loop(0, 4, join, 0)
    chip_of = lambda o: lax.rem(y + o, 4)
    parts = [
        remote(part_tx.at[chip_of(o)], part_rx.at[y], s_part, o, (c, 2 * chip_of(o) + k))
        for o in range(1, 4)
    ]
    for cp in parts:
        cp.start()
    for cp in qs:
        cp.start()
    part_rx[pl.ds(y, 1)] = part_tx[pl.ds(y, 1)]

    for cp in kvs:
        cp.wait_recv()
    kv_load.wait()
    here_kv = kv.at[pl.ds(32, 16)]
    halos = [
        remote(here_kv, kv.at[pl.ds(16, 16)], s_halo, 0, (ctx_of(1), h)),
        remote(here_kv, kv.at[pl.ds(0, 16)], s_halo, 1, (ctx_of(2), h)),
    ]
    halos[0].start()

    for cp in parts:
        cp.wait_recv()
    total, through = get_message(part_rx.at[0])
    for i in range(1, 4):
        state, factor = get_message(part_rx.at[i])
        total = factor * total + state
        through = factor * through
    put_message(ctx_tx, total, through)
    steps = [
        remote(ctx_tx, near, s_ctx, 0, (ctx_of(1), h)),
        remote(ctx_tx, far, s_ctx, 1, (ctx_of(2), h)),
    ]
    for cp in steps:
        cp.start()

    def fill(i, _):
        mask_pos = column_of_positions(((c - 2) * shard + i * BLK).astype(F32), BLK)
        in_doc = (mask_pos >= starts[...]) & (mask_pos < ends[...])
        mask[i] = jnp.where(in_doc, 0.0, NEG).astype(BF16)
        return 0

    lax.fori_loop(0, (WINDOW + shard) // BLK, fill, 0)
    for cp in steps:
        cp.wait_recv()
    halos[1].start()
    near_s, near_f = get_message(near)
    state = near_s + near_f * get_message(far)[0]
    for i in range(4):
        ret_tx[i] = state.astype(BF16)
        if i < 3:
            part_s, part_f = get_message(part_rx.at[i])
            state = part_f * state + part_s
    rets = [
        remote(ret_tx.at[chip_of(o)], ret_rx.at[y], s_ret, o, (c, 2 * chip_of(o) + k))
        for o in range(1, 4)
    ]
    for cp in rets:
        cp.start()
    ret_rx[pl.ds(y, 1)] = ret_tx[pl.ds(y, 1)]
    for cp in rets:
        cp.wait_recv()

    def spread(i, _):
        s1 = ret_rx[i].astype(F32)
        s2 = own_f[i] * s1 + own_s[i]
        entering[pl.ds(4 * k + i, 1)] = jnp.where(k == 0, s1, s2).astype(BF16)[None]
        back_tx[i] = jnp.where(k == 0, s2, s1).astype(BF16)
        return 0

    lax.fori_loop(0, 4, spread, 0)
    back = remote(back_tx, entering.at[pl.ds(pl.multiple_of(4 * k, 4), 4)], s_back, 0, partner)
    back.start()
    z_load.wait()
    back.wait_recv()

    def finish(g):
        lanes_g = pl.ds(pl.multiple_of(g * width, width), width)
        heads = pl.ds(pl.multiple_of(g * 16, 16), 16)
        p = par[g]
        b_rows, c_rows = bcc[g, :, :NS], bcc[g, :, NS:]
        pairs = (dot(c_rows, b_rows, 1, 1) * inside[...]).astype(BF16)
        c_joined = jnp.where(joined, c_rows.astype(F32), 0.0).astype(BF16)
        mixed = dot(
            jnp.concatenate([pairs, c_joined], 1),
            jnp.concatenate([scaled[g], entering[g]], 0),
            1,
            0,
        )
        growth = expand(jnp.exp(cum_t[heads, :]), lanes2)
        ssm = mixed * growth + p[6:7] * xc[g].astype(F32)
        out_tx[g] = gate_norm(ssm, zbuf[:, lanes_g], p[4:5])

    def out_copy(o):
        g = head_of(o)
        return remote(out_tx.at[g], mamba_out.at[mine], s_out, o, (c, g))

    def send_group(o, _):
        finish(head_of(o))
        out_copy(o).start()
        return 0

    lax.fori_loop(1, n_head, send_group, 0)
    finish(h)
    own_out = pltpu.make_async_copy(out_tx.at[h], mamba_out.at[mine], local.at[5])
    own_out.start()

    for cp in qs:
        cp.wait_recv()
    q_load.wait()
    for cp in halos:
        cp.wait_recv()
    block_rows = pl.ds(pl.multiple_of(c * BLK, BLK), BLK)

    def attn_copy(o):
        d = ctx_of(o)
        return remote(attn_tx.at[d], attn_out.at[block_rows], s_attn, o, (d, h))

    def attn_block(o, _):
        d = ctx_of(o)
        b = order[d]
        q_rows = q[b]
        block_first = (c * shard + b * BLK).astype(F32)
        attn_tx[d] = attend(q_rows, WINDOW // BLK + b, block_first, starts[...], ends[...], kv, mask)

        @pl.when(o < n_ctx)
        def _():
            attn_copy(o).start()

        return 0

    lax.fori_loop(1, n_ctx + 1, attn_block, 0)
    own_attn = pltpu.make_async_copy(attn_tx.at[c], attn_out.at[block_rows], local.at[6])
    own_attn.start()

    own_out.wait()
    own_attn.wait()
    for cp in rims + pars + kvs + qs + [pair] + parts + halos + steps + rets + [back]:
        cp.wait_send()
    for o in range(1, n_head):
        out_copy(o).wait()
    for o in range(1, n_ctx):
        attn_copy(o).wait()


def shards(
    q_in, kv_in, x_in, z_in, bc_in, dt_in, conv_x, conv_bc, a_log, d_skip, norm_gain, doc_lengths, assign
):
    c = lax.axis_index("ctx")
    count = doc_lengths.shape[0]
    before = jnp.arange(count)[None, :] < jnp.arange(count)[:, None]
    begins = jnp.sum(jnp.where(before, doc_lengths[None, :], 0), axis=1)
    pad = (0, 128 - count)
    starts = jnp.pad(begins.astype(F32), pad, constant_values=1e9)[None]
    ends = jnp.pad((begins + doc_lengths).astype(F32), pad, constant_values=1e9)[None]
    to = lax.dynamic_index_in_dim(assign, c, 0, keepdims=False)
    index = jnp.arange(to.shape[0], dtype=jnp.int32)
    order = jnp.sum(jnp.where(to[None, :] == index[:, None], index[None, :], 0), axis=1)
    any_space = pl.BlockSpec(memory_space=pl.ANY)
    vmem = pl.BlockSpec(memory_space=pltpu.VMEM)
    buf = lambda *shape: pltpu.VMEM(shape, BF16)
    buf32 = lambda *shape: pltpu.VMEM(shape, F32)
    sems = lambda n: pltpu.SemaphoreType.DMA((2, n))
    return pl.pallas_call(
        layer_kernel,
        out_shape=(
            jax.ShapeDtypeStruct((2048, 1024), BF16),
            jax.ShapeDtypeStruct((2048, 512), BF16),
        ),
        in_specs=[pl.BlockSpec(memory_space=pltpu.SMEM)] + [any_space] * 5 + [vmem] * 8,
        out_specs=(any_space, any_space),
        scratch_shapes=[
            buf(272, 8192), buf(256, 8192), buf(272, 2048), buf(8, 256, 1024), buf(8, 256, 1024),
            buf(8, 256, 256), buf32(8, 8, 1024), buf32(128, 256), buf32(128, 256), buf32(256, 256),
            buf32(4, NS, 1024), buf32(4, 1, 1024), buf(4, MSG, 1024), buf(4, MSG, 1024),
            buf(4, MSG, 1024), buf(4, MSG, 1024), buf(MSG, 1024), buf(MSG, 1024), buf(MSG, 1024),
            buf(4, NS, 1024), buf(4, NS, 1024), buf(4, NS, 1024), buf(8, NS, 1024),
            buf(48, BLK, 256), buf(48, BLK, 128), buf(16, BLK, 512), buf(8, 256, 1024), buf(16, BLK, 512),
            pltpu.SemaphoreType.DMA((7,)), sems(8), sems(8), sems(8), sems(2), sems(2), sems(1),
            sems(4), sems(2), sems(4), sems(1), sems(8), sems(16),
        ],
        compiler_params=pltpu.CompilerParams(
            collective_id=0, has_side_effects=True, vmem_limit_bytes=VMEM_LIMIT
        ),
        cost_estimate=pl.CostEstimate(flops=40 << 30, bytes_accessed=32 << 20, transcendentals=48 << 20),
        name="layer",
    )(
        order, q_in.reshape(2, BLK, 4096), kv_in.reshape(2, BLK, 2048), x_in, z_in, bc_in, dt_in, conv_x, conv_bc, a_log[None], d_skip[None],
        norm_gain[None], starts, ends,
    )


def solution(mesh):
    rows = P(("ctx", "head"), None)
    return jax.shard_map(
        shards,
        mesh=mesh,
        in_specs=(rows,) * 6 + (P(None, "head"),) * 2 + (P("head"),) * 3 + (P(), P()),
        out_specs=(P("ctx", "head"), P("ctx", "head")),
        check_vma=False,
    )
```

```python
import functools
import math

import jax
import jax.numpy as jnp
from jax import lax
from jax.experimental import pallas as pl
from jax.experimental.pallas import tpu as pltpu
from jax.sharding import PartitionSpec as P

HEAD_SIZE = 128
MP = 64
NS = 128
BLK = 128
L = 256
EPS = 1e-05
NEG = -1e30
F32 = jnp.float32
BF16 = jnp.bfloat16
VMEM_LIMIT = 60 << 20
MESH = pl.DeviceIdType.MESH
TILE = 1024
WINDOW = 4096
SCALE2 = math.log2(math.e) / math.sqrt(HEAD_SIZE)
MSG = NS + 16


def dot(a, b, ca, cb, precision=None):
    return lax.dot_general(
        a, b, (((ca,), (cb,)), ((), ())), preferred_element_type=F32, precision=precision
    )


def silu(v):
    half = 0.5 * v
    return half + half * jnp.tanh(half)


def start_of(pos_col, starts_row):
    return jnp.max(jnp.where(starts_row <= pos_col, starts_row, 0.0), axis=1, keepdims=True)


def column_of_positions(first, count):
    return lax.broadcasted_iota(jnp.int32, (count, 1), 0).astype(F32) + first


def conv(rows, taps, offset):
    count = rows.shape[0] - 16
    total = rows[16:] * taps[3]
    for k in range(3):
        term = rows[13 + k : 13 + k + count] * taps[k]
        total = total + jnp.where(offset >= float(3 - k), term, 0.0)
    return silu(total)


def head_lanes(heads, width):
    lane = lax.broadcasted_iota(jnp.int32, (heads, width), 1) // MP
    row = lax.broadcasted_iota(jnp.int32, (heads, width), 0)
    return (lane == row).astype(F32)


def expand(values_t, lanes2):
    hi = values_t.astype(BF16)
    lo = (values_t - hi.astype(F32)).astype(BF16)
    return dot(jnp.concatenate([hi, lo], 0), lanes2, 0, 0)


def gate_norm(ssm, z, gain):
    gated = ssm * silu(z.astype(F32))
    mean_sq = jnp.mean(gated * gated, axis=1, keepdims=True)
    return (gated * lax.rsqrt(mean_sq + EPS) * gain).astype(BF16)


def put_message(ref, state, factor):
    ref[:NS] = state.astype(BF16)
    hi = factor.astype(BF16).astype(F32)
    row = lax.broadcasted_iota(jnp.int32, (16, state.shape[1]), 0)
    ref[NS:] = jnp.where(row == 0, hi, jnp.where(row == 1, factor - hi, 0.0)).astype(BF16)


def get_message(ref):
    tail = ref[NS:].astype(F32)
    return ref[:NS].astype(F32), tail[0:1] + tail[1:2]


def attend(q_rows, here, first, starts, ends, kv, mask):
    groups = q_rows.shape[1] // HEAD_SIZE
    queries = jnp.concatenate(
        [q_rows[:, i * HEAD_SIZE : (i + 1) * HEAD_SIZE] for i in range(groups)], 0
    )
    pos = column_of_positions(first, BLK)
    own = ((pos >= starts) & (pos < ends)).astype(F32).astype(BF16)
    queries = jnp.concatenate([queries, jnp.concatenate([own] * groups, 0)], 1)

    def scores_of(at, count):
        keys = [jnp.concatenate([kv[at + i][:, :HEAD_SIZE], mask[at + i]], 1) for i in range(count)]
        return dot(queries, jnp.concatenate(keys, 0), 1, 1)

    def mixed(probs, at, count):
        ones = jnp.ones((BLK, HEAD_SIZE), BF16)
        values = [jnp.concatenate([kv[at + i][:, HEAD_SIZE:], ones], 1) for i in range(count)]
        return dot(probs.astype(BF16), jnp.concatenate(values, 0), 1, 0)

    s = scores_of(here, 1)
    row = lax.broadcasted_iota(jnp.int32, s.shape, 0) % BLK
    col = lax.broadcasted_iota(jnp.int32, s.shape, 1)
    s = jnp.where(col <= row, s, NEG)
    peak = jnp.max(s, axis=1, keepdims=True)
    total = mixed(jnp.exp2((s - peak) * SCALE2), here, 1)
    for i in range(WINDOW // TILE):
        at = here - (i + 1) * (TILE // BLK)
        s = scores_of(at, TILE // BLK)
        new = jnp.maximum(peak, jnp.max(s, axis=1, keepdims=True))
        probs = jnp.exp2((s - new) * SCALE2)
        total = total * jnp.exp2((peak - new) * SCALE2) + mixed(probs, at, TILE // BLK)
        peak = new
    out = total[:, :HEAD_SIZE] / total[:, HEAD_SIZE:]
    return jnp.concatenate([out[i * BLK : (i + 1) * BLK] for i in range(groups)], 1).astype(BF16)


def remote(src, dst, sems, send_slot, recv_slot, device):
    return pltpu.make_async_remote_copy(
        src, dst, sems.at[0, send_slot], sems.at[1, recv_slot], device_id=device, device_id_type=MESH
    )


def layer_kernel(
    assign, q_in, kv_in, x_in, z_in, bc_in, dt_in, conv_x, conv_bc, a_log, d_skip, norm_gain, lengths,
    mamba_out, attn_out,
    xbuf, zbuf, bcbuf, xc, scaled, bcc, par, dt_t, cum_t, inside, own_s, own_f, pair_tx, pair_rx, part_tx,
    part_rx, ctx_tx, near, far, ret_tx, ret_rx, back_tx, entering, kv, mask, q, out_tx, attn_tx, starts, ends,
    local, s_kv, s_q, s_par, s_rim, s_halo, s_pair, s_part, s_ctx, s_ret, s_back, s_out, s_attn,
):
    c = lax.axis_index("ctx")
    h = lax.axis_index("head")
    n_ctx, n_head = 16, 8
    y, k = h // 2, h % 2
    rows, width = 256, 1024
    shard = rows * n_head
    nh, nc = lax.rem(h + 1, n_head), lax.rem(c + (h + 1) // n_head, n_ctx)
    ph, pc = lax.rem(h + n_head - 1, n_head), lax.rem(c + n_ctx - (n_head - h) // n_head, n_ctx)
    head_of = lambda o: lax.rem(h + o, n_head)
    ctx_of = lambda o: lax.rem(c + o, n_ctx)
    chip_of = lambda o: lax.rem(y + o, 4)
    chip_device = lambda i: (c, 2 * i + k)
    partner = (c, 2 * y + (1 - k))

    barrier = pltpu.get_barrier_semaphore()
    for o in range(1, n_head):
        pl.semaphore_signal(barrier, inc=1, device_id=(c, head_of(o)), device_id_type=MESH)
    for o in range(1, n_ctx):
        pl.semaphore_signal(barrier, inc=1, device_id=(ctx_of(o), h), device_id_type=MESH)
    pl.semaphore_signal(barrier, inc=1, device_id=(nc, nh), device_id_type=MESH)
    pl.semaphore_signal(barrier, inc=1, device_id=(pc, ph), device_id_type=MESH)

    x_load = pltpu.make_async_copy(x_in, xbuf.at[pl.ds(16, rows)], local.at[0])
    bc_load = pltpu.make_async_copy(bc_in, bcbuf.at[pl.ds(16, rows)], local.at[1])
    z_load = pltpu.make_async_copy(z_in, zbuf, local.at[2])
    mine = pl.ds(pl.multiple_of(h * rows, rows), rows)
    q_mine = pl.ds(2 * h, 2)
    kv_mine = pl.ds(WINDOW // BLK + 2 * h, 2)
    q_load = pltpu.make_async_copy(
        q_in.at[:, :, pl.ds(pl.multiple_of(h * 512, 512), 512)], q.at[q_mine], local.at[3]
    )
    kv_load = pltpu.make_async_copy(
        kv_in.at[:, :, pl.ds(pl.multiple_of(h * 256, 256), 256)], kv.at[kv_mine], local.at[4]
    )
    bc_load.start()
    x_load.start()

    lanes = head_lanes(16, width)
    lanes2 = jnp.concatenate([lanes, lanes], 0).astype(BF16)
    par[pl.ds(h, 1)] = jnp.zeros((1, 8, width), F32)
    own_par = par.at[h]
    own_par[0:4] = conv_x[...]
    own_par[4:5] = norm_gain[...]
    for i in range(4):
        own_par[5:6, i * 256 : (i + 1) * 256] = conv_bc[i : i + 1]
    skip8 = jnp.broadcast_to(d_skip[...], (8, 16))
    own_par[6:7] = dot(skip8, lanes, 1, 0, lax.Precision.HIGHEST)[0:1]
    own_par[7:8, 0:16] = a_log[...]

    pl.semaphore_wait(barrier, n_head - 1 + n_ctx - 1 + 2)

    rims = [
        remote(x_in.at[pl.ds(rows - 16, 16)], xbuf.at[pl.ds(0, 16)], s_rim, 0, 0, (nc, nh)),
        remote(bc_in.at[pl.ds(rows - 16, 16)], bcbuf.at[pl.ds(0, 16)], s_rim, 1, 1, (nc, nh)),
    ]
    pars = [remote(par.at[h], par.at[h], s_par, o, o, (c, head_of(o))) for o in range(1, n_head)]
    kvs = [
        remote(
            kv_in.at[:, :, pl.ds(pl.multiple_of(head_of(o) * 256, 256), 256)],
            kv.at[kv_mine], s_kv, o, o, (c, head_of(o)),
        )
        for o in range(1, n_head)
    ]
    qs = [
        remote(
            q_in.at[:, :, pl.ds(pl.multiple_of(head_of(o) * 512, 512), 512)],
            q.at[q_mine], s_q, o, o, (c, head_of(o)),
        )
        for o in range(1, n_head)
    ]
    for cp in rims + pars + kvs:
        cp.start()
    kv_load.start()
    q_load.start()
    z_load.start()

    count = lengths.shape[1]
    doc = lax.broadcasted_iota(jnp.int32, (count, 128), 0)
    lane = lax.broadcasted_iota(jnp.int32, (count, 128), 1)
    lengths8 = jnp.broadcast_to(lengths[...].astype(F32), (8, count))
    exact = lax.Precision.HIGHEST
    real = lane[0:1] < count
    begin = dot(lengths8, (doc < lane).astype(F32), 1, 0, exact)[0:1]
    starts[...] = jnp.where(real, begin, 1e9)
    ends[...] = jnp.where(real, dot(lengths8, (doc <= lane).astype(F32), 1, 0, exact)[0:1], 1e9)

    first = (c * shard + h * rows).astype(F32)
    pos = column_of_positions(first, rows)
    start = start_of(pos, starts[...])
    offset = pos - start
    row = lax.broadcasted_iota(jnp.int32, (rows, rows), 0)
    col = lax.broadcasted_iota(jnp.int32, (rows, rows), 1)
    inside[...] = ((col <= row) & (col.astype(F32) >= start - first)).astype(F32)
    joined = start < first
    joined_last = jnp.where(start[rows - 1 :] < first, 1.0, 0.0)
    in_last = pos >= start[rows - 1 :]
    upper = (row <= col).astype(F32)
    dt_t[...] = jnp.transpose(dt_in[...].astype(F32))

    for cp in pars:
        cp.wait_recv()
    a_col = jnp.concatenate(
        [jnp.transpose(par[g, :, 0:128])[0:16, 7:8] for g in range(n_head)], 0
    )
    cum_t[...] = dot(-jnp.exp(a_col) * dt_t[...], upper, 1, 0, exact)
    bc_load.wait()
    x_load.wait()
    for cp in rims:
        cp.wait_recv()

    def local_state(g):
        lanes_g = pl.ds(pl.multiple_of(g * width, width), width)
        p = par[g]
        x_rows = conv(
            xbuf[:, lanes_g].astype(F32), [p[i : i + 1] for i in range(4)], offset
        ).astype(BF16)
        bc_rows = conv(
            bcbuf[:, pl.ds(pl.multiple_of(g * 256, 256), 256)].astype(F32),
            [p[5:6, i * 256 : (i + 1) * 256] for i in range(4)],
            offset,
        )
        xc[g] = x_rows
        bcc[g] = bc_rows.astype(BF16)
        heads = pl.ds(pl.multiple_of(g * 16, 16), 16)
        cum = cum_t[heads, :]
        x_scaled = (x_rows.astype(F32) * expand(jnp.exp(-cum) * dt_t[heads, :], lanes2)).astype(BF16)
        scaled[g] = x_scaled
        growth = expand(jnp.exp(cum[:, rows - 128 :]), lanes2)[127:128]
        b_last = jnp.where(in_last, bc_rows[:, :NS], 0.0).astype(BF16)
        return growth * dot(b_last, x_scaled, 0, 0), growth * joined_last

    def pair_copy(i):
        return remote(pair_tx.at[i], pair_rx.at[i], s_pair, i, i, partner)

    def part_copy(i):
        return remote(part_tx.at[i], part_rx.at[y], s_part, i, y, chip_device(i))

    def other_side(n, _):
        i = chip_of(n)
        put_message(pair_tx.at[i], *local_state(4 * (1 - k) + i))
        pair_copy(i).start()
        return 0

    def own_side(n, _):
        i = chip_of(n)
        state, factor = local_state(4 * k + i)
        pair_copy(i).wait_recv()
        got_s, got_f = get_message(pair_rx.at[i])
        s1, f1 = jnp.where(k == 0, state, got_s), jnp.where(k == 0, factor, got_f)
        s2, f2 = jnp.where(k == 0, got_s, state), jnp.where(k == 0, got_f, factor)
        own_s[i] = s1
        own_f[i] = f1
        put_message(part_tx.at[i], f2 * s1 + s2, f2 * f1)

        @pl.when(n < 4)
        def _():
            part_copy(i).start()

        return 0

    lax.fori_loop(1, 5, other_side, 0)
    lax.fori_loop(1, 5, own_side, 0)
    part_rx[pl.ds(y, 1)] = part_tx[pl.ds(y, 1)]

    for cp in kvs:
        cp.wait_recv()
    kv_load.wait()
    here_kv = kv.at[pl.ds(32, 16)]
    halos = [
        remote(here_kv, kv.at[pl.ds(16, 16)], s_halo, 0, 0, (ctx_of(1), h)),
        remote(here_kv, kv.at[pl.ds(0, 16)], s_halo, 1, 1, (ctx_of(2), h)),
    ]
    halos[0].start()

    def fill(i, _):
        mask_pos = column_of_positions(((c - 2) * shard + i * BLK).astype(F32), BLK)
        in_doc = (mask_pos >= starts[...]) & (mask_pos < ends[...])
        mask[i] = jnp.where(in_doc, 0.0, NEG).astype(BF16)
        return 0

    lax.fori_loop(0, (WINDOW + shard) // BLK, fill, 0)

    def part_wait(i):
        remote(part_tx.at[i], part_rx.at[i], s_part, i, i, partner).wait_recv()

    for o in range(1, 4):
        part_wait(chip_of(o))
    for cp in qs:
        cp.start()
    total, through = get_message(part_rx.at[0])
    for i in range(1, 4):
        state, factor = get_message(part_rx.at[i])
        total = factor * total + state
        through = factor * through
    put_message(ctx_tx, total, through)
    steps = [
        remote(ctx_tx, near, s_ctx, 0, 0, (ctx_of(1), h)),
        remote(ctx_tx, far, s_ctx, 1, 1, (ctx_of(2), h)),
    ]
    for cp in steps:
        cp.start()
    for cp in steps:
        cp.wait_recv()
    halos[1].start()

    def ret_copy(i):
        return remote(ret_tx.at[i], ret_rx.at[y], s_ret, i, y, chip_device(i))

    near_s, near_f = get_message(near)
    state = near_s + near_f * get_message(far)[0]
    for i in range(4):
        ret_tx[i] = state.astype(BF16)

        @pl.when(y != i)
        def _():
            ret_copy(i).start()

        if i < 3:
            part_s, part_f = get_message(part_rx.at[i])
            state = part_f * state + part_s
    ret_rx[pl.ds(y, 1)] = ret_tx[pl.ds(y, 1)]

    def finish(g):
        lanes_g = pl.ds(pl.multiple_of(g * width, width), width)
        heads = pl.ds(pl.multiple_of(g * 16, 16), 16)
        p = par[g]
        b_rows, c_rows = bcc[g, :, :NS], bcc[g, :, NS:]
        pairs = (dot(c_rows, b_rows, 1, 1) * inside[...]).astype(BF16)
        c_joined = jnp.where(joined, c_rows.astype(F32), 0.0).astype(BF16)
        mixed = dot(
            jnp.concatenate([pairs, c_joined], 1),
            jnp.concatenate([scaled[g], entering[g]], 0),
            1,
            0,
        )
        growth = expand(jnp.exp(cum_t[heads, :]), lanes2)
        ssm = mixed * growth + p[6:7] * xc[g].astype(F32)
        out_tx[g] = gate_norm(ssm, zbuf[:, lanes_g], p[4:5])

        @pl.when(g != h)
        def _():
            out_copy(g).start()

    def out_copy(g):
        return remote(out_tx.at[g], mamba_out.at[mine], s_out, g, h, (c, g))

    def back_copy(i, side):
        slot = entering.at[4 * side + i]
        return remote(back_tx.at[i], slot, s_back, i, i, partner)

    z_load.wait()

    def own_groups(n, _):
        i = chip_of(n)

        @pl.when(n < 4)
        def _():
            remote(ret_tx.at[i], ret_rx.at[i], s_ret, i, i, partner).wait_recv()

        s1 = ret_rx[i].astype(F32)
        s2 = own_f[i] * s1 + own_s[i]
        entering[4 * k + i] = jnp.where(k == 0, s1, s2).astype(BF16)
        back_tx[i] = jnp.where(k == 0, s2, s1).astype(BF16)
        back_copy(i, k).start()
        finish(4 * k + i)
        return 0

    def other_groups(n, _):
        i = chip_of(n)
        back_copy(i, 1 - k).wait_recv()
        finish(4 * (1 - k) + i)
        return 0

    lax.fori_loop(1, 5, own_groups, 0)
    lax.fori_loop(1, 5, other_groups, 0)
    own_out = pltpu.make_async_copy(out_tx.at[h], mamba_out.at[mine], local.at[5])
    own_out.start()

    for cp in qs:
        cp.wait_recv()
    q_load.wait()
    for cp in halos:
        cp.wait_recv()
    block_rows = pl.ds(pl.multiple_of(c * BLK, BLK), BLK)

    def attn_copy(o):
        d = ctx_of(o)
        return remote(attn_tx.at[d], attn_out.at[block_rows], s_attn, o, o, (d, h))

    def attn_block(o, _):
        d = ctx_of(o)
        b = jnp.int32(0)
        for i in range(n_ctx):
            b = b + jnp.where(assign[c, i] == d, i, 0)
        b = jnp.minimum(b, n_ctx - 1)
        block_first = (c * shard + b * BLK).astype(F32)
        attn_tx[d] = attend(q[b], WINDOW // BLK + b, block_first, starts[...], ends[...], kv, mask)

        @pl.when(o < n_ctx)
        def _():
            attn_copy(o).start()

        return 0

    lax.fori_loop(1, n_ctx + 1, attn_block, 0)
    own_attn = pltpu.make_async_copy(attn_tx.at[c], attn_out.at[block_rows], local.at[6])
    own_attn.start()

    own_out.wait()
    own_attn.wait()
    for cp in rims + pars + kvs + qs + halos + steps:
        cp.wait_send()
    for i in range(4):
        pair_copy(i).wait_send()
        back_copy(i, k).wait_send()
    for o in range(1, 4):
        part_copy(chip_of(o)).wait_send()
        ret_copy(chip_of(o)).wait_send()
    for o in range(1, n_head):
        out_copy(head_of(o)).wait_send()
        remote(out_tx.at[h], mamba_out.at[mine], s_out, h, head_of(o), partner).wait_recv()
    for o in range(1, n_ctx):
        attn_copy(o).wait()


def shards(
    q_in, kv_in, x_in, z_in, bc_in, dt_in, conv_x, conv_bc, a_log, d_skip, norm_gain, doc_lengths, assign
):
    any_space = pl.BlockSpec(memory_space=pl.ANY)
    vmem = pl.BlockSpec(memory_space=pltpu.VMEM)
    buf = lambda *shape: pltpu.VMEM(shape, BF16)
    buf32 = lambda *shape: pltpu.VMEM(shape, F32)
    sems = lambda n: pltpu.SemaphoreType.DMA((2, n))
    return pl.pallas_call(
        layer_kernel,
        out_shape=(
            jax.ShapeDtypeStruct((2048, 1024), BF16),
            jax.ShapeDtypeStruct((2048, 512), BF16),
        ),
        in_specs=[pl.BlockSpec(memory_space=pltpu.SMEM)] + [any_space] * 5 + [vmem] * 7,
        out_specs=(any_space, any_space),
        scratch_shapes=[
            buf(272, 8192), buf(256, 8192), buf(272, 2048), buf(8, 256, 1024), buf(8, 256, 1024),
            buf(8, 256, 256), buf32(8, 8, 1024), buf32(128, 256), buf32(128, 256), buf32(256, 256),
            buf32(4, NS, 1024), buf32(4, 1, 1024), buf(4, MSG, 1024), buf(4, MSG, 1024),
            buf(4, MSG, 1024), buf(4, MSG, 1024), buf(MSG, 1024), buf(MSG, 1024), buf(MSG, 1024),
            buf(4, NS, 1024), buf(4, NS, 1024), buf(4, NS, 1024), buf(8, NS, 1024),
            buf(48, BLK, 256), buf(48, BLK, 128), buf(16, BLK, 512), buf(8, 256, 1024), buf(16, BLK, 512),
            buf32(1, 128), buf32(1, 128),
            pltpu.SemaphoreType.DMA((7,)), sems(8), sems(8), sems(8), sems(2), sems(2), sems(4),
            sems(4), sems(2), sems(4), sems(4), sems(8), sems(16),
        ],
        compiler_params=pltpu.CompilerParams(
            collective_id=0, has_side_effects=True, vmem_limit_bytes=VMEM_LIMIT
        ),
        cost_estimate=pl.CostEstimate(flops=40 << 30, bytes_accessed=32 << 20, transcendentals=48 << 20),
        name="layer",
    )(
        assign, q_in.reshape(2, BLK, 4096), kv_in.reshape(2, BLK, 2048), x_in, z_in, bc_in, dt_in, conv_x, conv_bc, a_log[None], d_skip[None],
        norm_gain[None], doc_lengths[None],
    )


def solution(mesh):
    rows = P(("ctx", "head"), None)
    return jax.shard_map(
        shards,
        mesh=mesh,
        in_specs=(rows,) * 6 + (P(None, "head"),) * 2 + (P("head"),) * 3 + (P(), P()),
        out_specs=(P("ctx", "head"), P("ctx", "head")),
        check_vma=False,
    )
```

```python
import functools
import math

import jax
import jax.numpy as jnp
from jax import lax
from jax.experimental import pallas as pl
from jax.experimental.pallas import tpu as pltpu
from jax.sharding import PartitionSpec as P

HEAD_SIZE = 128
MP = 64
NS = 128
BLK = 128
L = 256
EPS = 1e-05
NEG = -1e30
F32 = jnp.float32
BF16 = jnp.bfloat16
VMEM_LIMIT = 60 << 20
MESH = pl.DeviceIdType.MESH
TILE = 1024
WINDOW = 4096
SCALE2 = math.log2(math.e) / math.sqrt(HEAD_SIZE)
MSG = NS + 16


def dot(a, b, ca, cb, precision=None):
    return lax.dot_general(
        a, b, (((ca,), (cb,)), ((), ())), preferred_element_type=F32, precision=precision
    )


def silu(v):
    half = 0.5 * v
    return half + half * jnp.tanh(half)


def start_of(pos_col, starts_row):
    return jnp.max(jnp.where(starts_row <= pos_col, starts_row, 0.0), axis=1, keepdims=True)


def column_of_positions(first, count):
    return lax.broadcasted_iota(jnp.int32, (count, 1), 0).astype(F32) + first


def conv(rows, taps, offset):
    count = rows.shape[0] - 16
    total = rows[16:] * taps[3]
    for k in range(3):
        term = rows[13 + k : 13 + k + count] * taps[k]
        total = total + jnp.where(offset >= float(3 - k), term, 0.0)
    return silu(total)


def head_lanes(heads, width):
    lane = lax.broadcasted_iota(jnp.int32, (heads, width), 1) // MP
    row = lax.broadcasted_iota(jnp.int32, (heads, width), 0)
    return (lane == row).astype(F32)


def expand(values_t, lanes2):
    hi = values_t.astype(BF16)
    lo = (values_t - hi.astype(F32)).astype(BF16)
    return dot(jnp.concatenate([hi, lo], 0), lanes2, 0, 0)


def gate_norm(ssm, z, gain):
    gated = ssm * silu(z.astype(F32))
    mean_sq = jnp.mean(gated * gated, axis=1, keepdims=True)
    return (gated * lax.rsqrt(mean_sq + EPS) * gain).astype(BF16)


def put_message(ref, state, factor):
    ref[:NS] = state.astype(BF16)
    hi = factor.astype(BF16).astype(F32)
    row = lax.broadcasted_iota(jnp.int32, (16, state.shape[1]), 0)
    ref[NS:] = jnp.where(row == 0, hi, jnp.where(row == 1, factor - hi, 0.0)).astype(BF16)


def get_message(ref):
    tail = ref[NS:].astype(F32)
    return ref[:NS].astype(F32), tail[0:1] + tail[1:2]


def attend(q_rows, here, first, starts, ends, kv, mask):
    groups = q_rows.shape[1] // HEAD_SIZE
    queries = jnp.concatenate(
        [q_rows[:, i * HEAD_SIZE : (i + 1) * HEAD_SIZE] for i in range(groups)], 0
    )
    pos = column_of_positions(first, BLK)
    own = ((pos >= starts) & (pos < ends)).astype(F32).astype(BF16)
    queries = jnp.concatenate([queries, jnp.concatenate([own] * groups, 0)], 1)

    def scores_of(at, count):
        keys = [jnp.concatenate([kv[at + i][:, :HEAD_SIZE], mask[at + i]], 1) for i in range(count)]
        return dot(queries, jnp.concatenate(keys, 0), 1, 1)

    def mixed(probs, at, count):
        ones = jnp.ones((BLK, HEAD_SIZE), BF16)
        values = [jnp.concatenate([kv[at + i][:, HEAD_SIZE:], ones], 1) for i in range(count)]
        return dot(probs.astype(BF16), jnp.concatenate(values, 0), 1, 0)

    s = scores_of(here, 1)
    row = lax.broadcasted_iota(jnp.int32, s.shape, 0) % BLK
    col = lax.broadcasted_iota(jnp.int32, s.shape, 1)
    s = jnp.where(col <= row, s, NEG)
    peak = jnp.max(s, axis=1, keepdims=True)
    total = mixed(jnp.exp2((s - peak) * SCALE2), here, 1)
    for i in range(WINDOW // TILE):
        at = here - (i + 1) * (TILE // BLK)
        s = scores_of(at, TILE // BLK)
        new = jnp.maximum(peak, jnp.max(s, axis=1, keepdims=True))
        probs = jnp.exp2((s - new) * SCALE2)
        total = total * jnp.exp2((peak - new) * SCALE2) + mixed(probs, at, TILE // BLK)
        peak = new
    out = total[:, :HEAD_SIZE] / total[:, HEAD_SIZE:]
    return jnp.concatenate([out[i * BLK : (i + 1) * BLK] for i in range(groups)], 1).astype(BF16)


def remote(src, dst, sems, send_slot, recv_slot, device):
    return pltpu.make_async_remote_copy(
        src, dst, sems.at[0, send_slot], sems.at[1, recv_slot], device_id=device, device_id_type=MESH
    )


def layer_kernel(
    assign, q_in, kv_in, x_in, z_in, bc_in, dt_in, conv_x, conv_bc, a_log, d_skip, norm_gain, lengths,
    mamba_out, attn_out,
    xbuf, zbuf, bcbuf, xc, scaled, bcc, par, dt_t, cum_t, inside, own_s, own_f, pair_tx, pair_rx, part_tx,
    part_rx, ctx_tx, near, far, ret_tx, ret_rx, back_tx, entering, kv, mask, q, out_tx, attn_tx, starts, ends,
    local, s_kv, s_q, s_par, s_rim, s_halo, s_pair, s_part, s_ctx, s_ret, s_back, s_out, s_attn,
):
    c = lax.axis_index("ctx")
    h = lax.axis_index("head")
    n_ctx, n_head = 16, 8
    y, k = h // 2, h % 2
    rows, width = 256, 1024
    shard = rows * n_head
    nh, nc = lax.rem(h + 1, n_head), lax.rem(c + (h + 1) // n_head, n_ctx)
    ph, pc = lax.rem(h + n_head - 1, n_head), lax.rem(c + n_ctx - (n_head - h) // n_head, n_ctx)
    head_of = lambda o: lax.rem(h + o, n_head)
    ctx_of = lambda o: lax.rem(c + o, n_ctx)
    chip_of = lambda o: lax.rem(y + o, 4)
    chip_device = lambda i: (c, 2 * i + k)
    partner = (c, 2 * y + (1 - k))

    barrier = pltpu.get_barrier_semaphore()
    for o in range(1, n_head):
        pl.semaphore_signal(barrier, inc=1, device_id=(c, head_of(o)), device_id_type=MESH)
    for o in range(1, n_ctx):
        pl.semaphore_signal(barrier, inc=1, device_id=(ctx_of(o), h), device_id_type=MESH)
    pl.semaphore_signal(barrier, inc=1, device_id=(nc, nh), device_id_type=MESH)
    pl.semaphore_signal(barrier, inc=1, device_id=(pc, ph), device_id_type=MESH)

    x_load = pltpu.make_async_copy(x_in, xbuf.at[pl.ds(16, rows)], local.at[0])
    bc_load = pltpu.make_async_copy(bc_in, bcbuf.at[pl.ds(16, rows)], local.at[1])
    z_load = pltpu.make_async_copy(z_in, zbuf, local.at[2])
    mine = pl.ds(pl.multiple_of(h * rows, rows), rows)
    q_mine = pl.ds(2 * h, 2)
    kv_mine = pl.ds(WINDOW // BLK + 2 * h, 2)
    q_load = pltpu.make_async_copy(
        q_in.at[:, :, pl.ds(pl.multiple_of(h * 512, 512), 512)], q.at[q_mine], local.at[3]
    )
    kv_load = pltpu.make_async_copy(
        kv_in.at[:, :, pl.ds(pl.multiple_of(h * 256, 256), 256)], kv.at[kv_mine], local.at[4]
    )
    bc_load.start()
    x_load.start()

    lanes = head_lanes(16, width)
    lanes2 = jnp.concatenate([lanes, lanes], 0).astype(BF16)
    par[pl.ds(h, 1)] = jnp.zeros((1, 8, width), F32)
    own_par = par.at[h]
    own_par[0:4] = conv_x[...]
    own_par[4:5] = norm_gain[...]
    for i in range(4):
        own_par[5:6, i * 256 : (i + 1) * 256] = conv_bc[i : i + 1]
    skip8 = jnp.broadcast_to(d_skip[...], (8, 16))
    own_par[6:7] = dot(skip8, lanes, 1, 0, lax.Precision.HIGHEST)[0:1]
    own_par[7:8, 0:16] = a_log[...]

    pl.semaphore_wait(barrier, n_head - 1 + n_ctx - 1 + 2)

    rims = [
        remote(x_in.at[pl.ds(rows - 16, 16)], xbuf.at[pl.ds(0, 16)], s_rim, 0, 0, (nc, nh)),
        remote(bc_in.at[pl.ds(rows - 16, 16)], bcbuf.at[pl.ds(0, 16)], s_rim, 1, 1, (nc, nh)),
    ]
    pars = [remote(par.at[h], par.at[h], s_par, o, o, (c, head_of(o))) for o in range(1, n_head)]
    kvs = [
        remote(
            kv_in.at[:, :, pl.ds(pl.multiple_of(head_of(o) * 256, 256), 256)],
            kv.at[kv_mine], s_kv, o, o, (c, head_of(o)),
        )
        for o in range(1, n_head)
    ]
    qs = [
        remote(
            q_in.at[:, :, pl.ds(pl.multiple_of(head_of(o) * 512, 512), 512)],
            q.at[q_mine], s_q, o, o, (c, head_of(o)),
        )
        for o in range(1, n_head)
    ]
    for cp in rims + pars + kvs:
        cp.start()
    kv_load.start()
    q_load.start()
    z_load.start()

    count = lengths.shape[1]
    doc = lax.broadcasted_iota(jnp.int32, (count, 128), 0)
    lane = lax.broadcasted_iota(jnp.int32, (count, 128), 1)
    lengths8 = jnp.broadcast_to(lengths[...].astype(F32), (8, count))
    exact = lax.Precision.HIGHEST
    real = lane[0:1] < count
    begin = dot(lengths8, (doc < lane).astype(F32), 1, 0, exact)[0:1]
    starts[...] = jnp.where(real, begin, 1e9)
    ends[...] = jnp.where(real, dot(lengths8, (doc <= lane).astype(F32), 1, 0, exact)[0:1], 1e9)

    first = (c * shard + h * rows).astype(F32)
    pos = column_of_positions(first, rows)
    start = start_of(pos, starts[...])
    offset = pos - start
    row = lax.broadcasted_iota(jnp.int32, (rows, rows), 0)
    col = lax.broadcasted_iota(jnp.int32, (rows, rows), 1)
    inside[...] = ((col <= row) & (col.astype(F32) >= start - first)).astype(F32)
    joined = start < first
    joined_last = jnp.where(start[rows - 1 :] < first, 1.0, 0.0)
    in_last = pos >= start[rows - 1 :]
    upper = (row <= col).astype(F32)
    dt_t[...] = jnp.transpose(dt_in[...].astype(F32))

    for cp in pars:
        cp.wait_recv()
    a_col = jnp.concatenate(
        [jnp.transpose(par[g, :, 0:128])[0:16, 7:8] for g in range(n_head)], 0
    )
    cum_t[...] = dot(-jnp.exp(a_col) * dt_t[...], upper, 1, 0, exact)
    bc_load.wait()
    x_load.wait()
    for cp in rims:
        cp.wait_recv()

    def local_state(g):
        lanes_g = pl.ds(pl.multiple_of(g * width, width), width)
        p = par[g]
        x_rows = conv(
            xbuf[:, lanes_g].astype(F32), [p[i : i + 1] for i in range(4)], offset
        ).astype(BF16)
        bc_rows = conv(
            bcbuf[:, pl.ds(pl.multiple_of(g * 256, 256), 256)].astype(F32),
            [p[5:6, i * 256 : (i + 1) * 256] for i in range(4)],
            offset,
        )
        xc[g] = x_rows
        bcc[g] = bc_rows.astype(BF16)
        heads = pl.ds(pl.multiple_of(g * 16, 16), 16)
        cum = cum_t[heads, :]
        x_scaled = (x_rows.astype(F32) * expand(jnp.exp(-cum) * dt_t[heads, :], lanes2)).astype(BF16)
        scaled[g] = x_scaled
        growth = expand(jnp.exp(cum[:, rows - 128 :]), lanes2)[127:128]
        b_last = jnp.where(in_last, bc_rows[:, :NS], 0.0).astype(BF16)
        return growth * dot(b_last, x_scaled, 0, 0), growth * joined_last

    def pair_copy(i):
        return remote(pair_tx.at[i], pair_rx.at[i], s_pair, i, i, partner)

    def part_copy(i):
        return remote(part_tx.at[i], part_rx.at[y], s_part, i, y, chip_device(i))

    def other_side(n, _):
        i = chip_of(n)
        put_message(pair_tx.at[i], *local_state(4 * (1 - k) + i))
        pair_copy(i).start()
        return 0

    def own_side(n, _):
        i = chip_of(n)
        state, factor = local_state(4 * k + i)
        pair_copy(i).wait_recv()
        got_s, got_f = get_message(pair_rx.at[i])
        s1, f1 = jnp.where(k == 0, state, got_s), jnp.where(k == 0, factor, got_f)
        s2, f2 = jnp.where(k == 0, got_s, state), jnp.where(k == 0, got_f, factor)
        own_s[i] = s1
        own_f[i] = f1
        put_message(part_tx.at[i], f2 * s1 + s2, f2 * f1)

        @pl.when(n < 4)
        def _():
            part_copy(i).start()

        return 0

    lax.fori_loop(1, 5, other_side, 0)
    for cp in kvs:
        cp.wait_recv()
    kv_load.wait()
    here_kv = kv.at[pl.ds(32, 16)]
    halos = [
        remote(here_kv, kv.at[pl.ds(16, 16)], s_halo, 0, 0, (ctx_of(1), h)),
        remote(here_kv, kv.at[pl.ds(0, 16)], s_halo, 1, 1, (ctx_of(2), h)),
    ]
    halos[0].start()
    lax.fori_loop(1, 5, own_side, 0)
    part_rx[pl.ds(y, 1)] = part_tx[pl.ds(y, 1)]

    def fill(i, _):
        mask_pos = column_of_positions(((c - 2) * shard + i * BLK).astype(F32), BLK)
        in_doc = (mask_pos >= starts[...]) & (mask_pos < ends[...])
        mask[i] = jnp.where(in_doc, 0.0, NEG).astype(BF16)
        return 0

    lax.fori_loop(0, (WINDOW + shard) // BLK, fill, 0)

    def part_wait(i):
        remote(part_tx.at[i], part_rx.at[i], s_part, i, i, partner).wait_recv()

    for o in range(1, 4):
        part_wait(chip_of(o))
    for cp in qs:
        cp.start()
    total, through = get_message(part_rx.at[0])
    for i in range(1, 4):
        state, factor = get_message(part_rx.at[i])
        total = factor * total + state
        through = factor * through
    put_message(ctx_tx, total, through)
    steps = [
        remote(ctx_tx, near, s_ctx, 0, 0, (ctx_of(1), h)),
        remote(ctx_tx, far, s_ctx, 1, 1, (ctx_of(2), h)),
    ]
    for cp in steps:
        cp.start()
    for cp in steps:
        cp.wait_recv()
    halos[1].start()

    def ret_copy(i):
        return remote(ret_tx.at[i], ret_rx.at[y], s_ret, i, y, chip_device(i))

    near_s, near_f = get_message(near)
    state = near_s + near_f * get_message(far)[0]
    for i in range(4):
        ret_tx[i] = state.astype(BF16)

        @pl.when(y != i)
        def _():
            ret_copy(i).start()

        if i < 3:
            part_s, part_f = get_message(part_rx.at[i])
            state = part_f * state + part_s
    ret_rx[pl.ds(y, 1)] = ret_tx[pl.ds(y, 1)]

    def finish(g):
        lanes_g = pl.ds(pl.multiple_of(g * width, width), width)
        heads = pl.ds(pl.multiple_of(g * 16, 16), 16)
        p = par[g]
        b_rows, c_rows = bcc[g, :, :NS], bcc[g, :, NS:]
        pairs = (dot(c_rows, b_rows, 1, 1) * inside[...]).astype(BF16)
        c_joined = jnp.where(joined, c_rows.astype(F32), 0.0).astype(BF16)
        mixed = dot(
            jnp.concatenate([pairs, c_joined], 1),
            jnp.concatenate([scaled[g], entering[g]], 0),
            1,
            0,
        )
        growth = expand(jnp.exp(cum_t[heads, :]), lanes2)
        ssm = mixed * growth + p[6:7] * xc[g].astype(F32)
        out_tx[g] = gate_norm(ssm, zbuf[:, lanes_g], p[4:5])

        @pl.when(g != h)
        def _():
            out_copy(g).start()

    def out_copy(g):
        return remote(out_tx.at[g], mamba_out.at[mine], s_out, g, h, (c, g))

    def back_copy(i, side):
        slot = entering.at[4 * side + i]
        return remote(back_tx.at[i], slot, s_back, i, i, partner)

    z_load.wait()

    def own_groups(n, _):
        i = chip_of(n)

        @pl.when(n < 4)
        def _():
            remote(ret_tx.at[i], ret_rx.at[i], s_ret, i, i, partner).wait_recv()

        s1 = ret_rx[i].astype(F32)
        s2 = own_f[i] * s1 + own_s[i]
        entering[4 * k + i] = jnp.where(k == 0, s1, s2).astype(BF16)
        back_tx[i] = jnp.where(k == 0, s2, s1).astype(BF16)
        back_copy(i, k).start()
        finish(4 * k + i)
        return 0

    def other_groups(n, _):
        i = chip_of(n)
        back_copy(i, 1 - k).wait_recv()
        finish(4 * (1 - k) + i)
        return 0

    lax.fori_loop(1, 5, own_groups, 0)
    lax.fori_loop(1, 5, other_groups, 0)
    own_out = pltpu.make_async_copy(out_tx.at[h], mamba_out.at[mine], local.at[5])
    own_out.start()

    for cp in qs:
        cp.wait_recv()
    q_load.wait()
    for cp in halos:
        cp.wait_recv()
    block_rows = pl.ds(pl.multiple_of(c * BLK, BLK), BLK)

    def attn_copy(o):
        d = ctx_of(o)
        return remote(attn_tx.at[d], attn_out.at[block_rows], s_attn, o, o, (d, h))

    def attn_block(o, _):
        d = ctx_of(o)
        b = jnp.int32(0)
        for i in range(n_ctx):
            b = b + jnp.where(assign[c, i] == d, i, 0)
        b = jnp.minimum(b, n_ctx - 1)
        block_first = (c * shard + b * BLK).astype(F32)
        attn_tx[d] = attend(q[b], WINDOW // BLK + b, block_first, starts[...], ends[...], kv, mask)

        @pl.when(o < n_ctx)
        def _():
            attn_copy(o).start()

        return 0

    lax.fori_loop(1, n_ctx + 1, attn_block, 0)
    own_attn = pltpu.make_async_copy(attn_tx.at[c], attn_out.at[block_rows], local.at[6])
    own_attn.start()

    own_out.wait()
    own_attn.wait()
    for cp in rims + pars + kvs + qs + halos + steps:
        cp.wait_send()
    for i in range(4):
        pair_copy(i).wait_send()
        back_copy(i, k).wait_send()
    for o in range(1, 4):
        part_copy(chip_of(o)).wait_send()
        ret_copy(chip_of(o)).wait_send()
    for o in range(1, n_head):
        out_copy(head_of(o)).wait_send()
        remote(out_tx.at[h], mamba_out.at[mine], s_out, h, head_of(o), partner).wait_recv()
    for o in range(1, n_ctx):
        attn_copy(o).wait()


def shards(
    q_in, kv_in, x_in, z_in, bc_in, dt_in, conv_x, conv_bc, a_log, d_skip, norm_gain, doc_lengths, assign
):
    any_space = pl.BlockSpec(memory_space=pl.ANY)
    vmem = pl.BlockSpec(memory_space=pltpu.VMEM)
    buf = lambda *shape: pltpu.VMEM(shape, BF16)
    buf32 = lambda *shape: pltpu.VMEM(shape, F32)
    sems = lambda n: pltpu.SemaphoreType.DMA((2, n))
    return pl.pallas_call(
        layer_kernel,
        out_shape=(
            jax.ShapeDtypeStruct((2048, 1024), BF16),
            jax.ShapeDtypeStruct((2048, 512), BF16),
        ),
        in_specs=[pl.BlockSpec(memory_space=pltpu.SMEM)] + [any_space] * 5 + [vmem] * 7,
        out_specs=(any_space, any_space),
        scratch_shapes=[
            buf(272, 8192), buf(256, 8192), buf(272, 2048), buf(8, 256, 1024), buf(8, 256, 1024),
            buf(8, 256, 256), buf32(8, 8, 1024), buf32(128, 256), buf32(128, 256), buf32(256, 256),
            buf32(4, NS, 1024), buf32(4, 1, 1024), buf(4, MSG, 1024), buf(4, MSG, 1024),
            buf(4, MSG, 1024), buf(4, MSG, 1024), buf(MSG, 1024), buf(MSG, 1024), buf(MSG, 1024),
            buf(4, NS, 1024), buf(4, NS, 1024), buf(4, NS, 1024), buf(8, NS, 1024),
            buf(48, BLK, 256), buf(48, BLK, 128), buf(16, BLK, 512), buf(8, 256, 1024), buf(16, BLK, 512),
            buf32(1, 128), buf32(1, 128),
            pltpu.SemaphoreType.DMA((7,)), sems(8), sems(8), sems(8), sems(2), sems(2), sems(4),
            sems(4), sems(2), sems(4), sems(4), sems(8), sems(16),
        ],
        compiler_params=pltpu.CompilerParams(
            collective_id=0, has_side_effects=True, vmem_limit_bytes=VMEM_LIMIT
        ),
        cost_estimate=pl.CostEstimate(flops=40 << 30, bytes_accessed=32 << 20, transcendentals=48 << 20),
        name="layer",
    )(
        assign, q_in.reshape(2, BLK, 4096), kv_in.reshape(2, BLK, 2048), x_in, z_in, bc_in, dt_in, conv_x, conv_bc, a_log[None], d_skip[None],
        norm_gain[None], doc_lengths[None],
    )


def solution(mesh):
    rows = P(("ctx", "head"), None)
    return jax.shard_map(
        shards,
        mesh=mesh,
        in_specs=(rows,) * 6 + (P(None, "head"),) * 2 + (P("head"),) * 3 + (P(), P()),
        out_specs=(P("ctx", "head"), P("ctx", "head")),
        check_vma=False,
    )
```
